32 devices in a mesh: seq: 8 (over y, x, core), ch: 4 (over z).
Axes of the slice: x: 2, y: 2, z: 4, core: 2. Of those that a mesh axis runs over, the one named last changes fastest.
Arguments:
- query_feat: bfloat16 [8192, 4096], P('seq', 'ch'), may hold values from -6 to 6
- key_feat: bfloat16 [8192, 4096], P('seq', 'ch'), may hold values from -6 to 6
- value_feat: bfloat16 [8192, 4096], P('seq', 'ch'), may hold values from -6 to 6
- decay_rates: float32 [256, 16], P('ch'), may hold values from 2.4414063e-05 to 0.041666667
- residues: float32 [256, 16], P('ch'), may hold values from -0.28867513 to 0.28867513
- out_weight: bfloat16 [4096, 4096], P('ch', 'seq'), may hold values from -0.09375 to 0.09375
Outputs:
- mixed: bfloat16 [8192, 4096], P(('seq', 'ch'))
The draws below stay inside these ranges and needn't reach their ends.
All inputs are finite; a program needn't handle non-finite values.
Results may differ from the reference program's by a relative error of at most 0.014.
Values may be sent and summed in bfloat16 or wider, within the bound.
No kernel may reach another device: no remote copies, remote signals or barrier semaphores. Data moves between devices by JAX's collectives and lax.ppermute only.
A program may use at most 128 MiB of HBM per device.

```python
import math
import jax
import jax.numpy as jnp
import numpy as np
from jax import lax

D = 4096
MODES = 16
SUB = 256
SEQ_LEN = 8192
GROUPS = 256


def rate_table(key):
    slow_key, fast_key, pick_key = jax.random.split(jax.random.fold_in(key, 11), 3)
    slow = jnp.exp(jax.random.uniform(slow_key, (GROUPS, MODES), jnp.float32, math.log(0.2 / SEQ_LEN), math.log(2.0 / SEQ_LEN)))
    fast = jnp.exp(jax.random.uniform(fast_key, (GROUPS, MODES), jnp.float32, math.log(1.0 / 64), math.log(1.0 / 24)))
    share = 0.5
    picked = jax.random.uniform(pick_key, (GROUPS, MODES), jnp.float32) < share
    return jnp.clip(jnp.where(picked, slow, fast), 0.2 / SEQ_LEN, 1.0 / 24)


def draw_decay_rates(key, part):
    return rate_table(key).astype(jnp.float32)


def draw_residues(key, part):
    table = rate_table(key)
    noise_key = jax.random.fold_in(key, 23)
    noise = jax.random.truncated_normal(noise_key, -4.0, 4.0, (GROUPS, MODES), jnp.float32)
    return (noise * jnp.sqrt(2.0 * table / MODES)).astype(jnp.float32)


def block_levels(own_key, dims, pieces, least, top_value):
    def one(axis_at, parts):
        heights = jax.random.uniform(jax.random.fold_in(jax.random.fold_in(own_key, 6), axis_at), (parts,), jnp.float32, least / len(pieces), top_value / len(pieces))
        return jnp.repeat(jnp.exp(heights), dims[axis_at] // parts).reshape((-1,) + (1,) * (len(dims) - axis_at - 1))

    gain = one(*pieces[0])
    for cut in pieces[1:]:
        gain = gain * one(*cut)
    return gain


def bell_draw(own_key, dims, scale, bound, cuts=(), kind=jnp.bfloat16):
    array = scale * jax.random.normal(own_key, dims, jnp.float32)
    if cuts:
        array = array * block_levels(own_key, dims, cuts, -0.22, 0.18)
    return jnp.clip(array, -bound, bound).astype(kind)


def setup_inputs(seed: int = 0) -> dict:
    arg_keys = jax.random.split(jax.random.key(seed), 7)
    query_feat = bell_draw(arg_keys[0], (SEQ_LEN, D), 1.0, 6.0, ((0, 8), (1, 4)))
    key_feat = bell_draw(arg_keys[1], (SEQ_LEN, D), 1.0, 6.0, ((0, 8), (1, 4)))
    value_feat = bell_draw(arg_keys[2], (SEQ_LEN, D), 1.0, 6.0, ((0, 8), (1, 4)))
    decay_rates = draw_decay_rates(jax.random.fold_in(arg_keys[6], 71), 0)
    residues = draw_residues(jax.random.fold_in(arg_keys[6], 71), 0)
    out_weight = bell_draw(arg_keys[5], (D, D), D ** -0.5, 0.09375, ((0, 4), (1, 8)))
    return {"query_feat": query_feat, "key_feat": key_feat, "value_feat": value_feat, "decay_rates": decay_rates, "residues": residues, "out_weight": out_weight}


def lag_table(block):
    rows = np.arange(block)[:, None]
    cols = np.arange(block)[None, :]
    return rows - cols + block


def reference(query_feat, key_feat, value_feat, decay_rates, residues, out_weight):
    seq_rows, width = query_feat.shape
    group_count, mode_count = decay_rates.shape
    group_width = width // group_count
    block_count = seq_rows // SUB
    hi = lax.Precision.HIGHEST
    mixed_u = (key_feat.astype(jnp.float32) * value_feat.astype(jnp.float32)).astype(jnp.bfloat16)
    lag_steps = jnp.arange(SUB, dtype=jnp.float32)
    filter_taps = jnp.sum(residues[:, :, None] * jnp.exp(-decay_rates[:, :, None] * lag_steps), axis=1).astype(jnp.bfloat16)
    padded = jnp.concatenate([jnp.zeros((group_count, SUB), jnp.bfloat16), filter_taps], axis=1)
    toeplitz = padded[:, lag_table(SUB)].astype(jnp.float32)
    inject = jnp.exp(-decay_rates[:, :, None] * (SUB - 1.0 - lag_steps)).astype(jnp.bfloat16).astype(jnp.float32)
    readout = residues[:, :, None] * jnp.exp(-decay_rates[:, :, None] * (lag_steps + 1.0))
    step_decay = jnp.exp(-decay_rates * SUB).T[:, :, None]
    blocks_u = mixed_u.reshape(block_count, SUB, group_count, group_width)
    blocks_q = query_feat.reshape(block_count, SUB, group_count, group_width)

    def advance(state, inputs):
        block_u, block_q = inputs
        uf = block_u.astype(jnp.float32)
        local_part = jnp.einsum("gab,bgc->agc", toeplitz, uf, precision=hi)
        carried = jnp.einsum("gma,mgc->agc", readout, state, precision=hi)
        gated = (block_q.astype(jnp.float32) * (local_part + carried)).astype(jnp.bfloat16)
        block_sums = jnp.einsum("gmb,bgc->mgc", inject, uf, precision=hi)
        return step_decay * state + block_sums, gated

    start_state = jnp.zeros((mode_count, group_count, group_width), jnp.float32)
    _, gated_all = lax.scan(advance, start_state, (blocks_u, blocks_q))
    gated_all = gated_all.reshape(seq_rows, width)
    return jnp.dot(gated_all, out_weight, preferred_element_type=jnp.float32).astype(jnp.bfloat16)
```

```python
import functools

import jax
import jax.numpy as jnp
from jax import lax
from jax.experimental import pallas as pl
from jax.experimental.pallas import tpu as pltpu
from jax.sharding import PartitionSpec as P

SUB = 256
TILE = 128
F32 = jnp.float32
BF16 = jnp.bfloat16


def dot32(a, b):
    return jnp.dot(a, b, preferred_element_type=F32)


def own_mask(rows, cols, modes, width):
    r = lax.broadcasted_iota(jnp.int32, (rows, cols), 0) // modes
    c = lax.broadcasted_iota(jnp.int32, (rows, cols), 1) // width
    return r == c


def range_state_kernel(modes, width, k_ref, v_ref, rate_ref, u_ref, f_ref):
    u = (k_ref[...].astype(F32) * v_ref[...].astype(F32)).astype(BF16)
    u_ref[...] = u
    toks, cols = u.shape
    rows = rate_ref.shape[0]
    left = (toks - 1) - lax.broadcasted_iota(jnp.int32, (rows, toks), 1)
    inject = jnp.exp(-rate_ref[...] * left.astype(F32)).astype(BF16)
    sums = jnp.where(own_mask(rows, cols, modes, width), dot32(inject, u), 0.0)
    f_ref[...] = jnp.sum(sums.reshape(rows // modes, modes, cols), axis=0).astype(BF16)


def range_state(key_feat, value_feat, rate_col, modes, width):
    toks, chans = key_feat.shape
    step = 256
    rows = step // width * modes
    feat = pl.BlockSpec((toks, step), lambda i: (0, i))
    return pl.pallas_call(
        functools.partial(range_state_kernel, modes, width),
        grid=(chans // step,),
        in_specs=[feat, feat, pl.BlockSpec((rows, 1), lambda i: (i, 0))],
        out_specs=[feat, pl.BlockSpec((modes, step), lambda i: (0, i))],
        out_shape=[
            jax.ShapeDtypeStruct((toks, chans), BF16),
            jax.ShapeDtypeStruct((modes, chans), BF16),
        ],
        compiler_params=pltpu.CompilerParams(vmem_limit_bytes=24 << 20),
        name="range_state",
    )(key_feat, value_feat, rate_col)


def local_kernel(
    modes, width, u_ref, rate_ref, res_ref, rate_row_ref, res_row_ref, z_ref, taps_ref
):
    groups = TILE // width
    rows = groups * modes
    rate, res = rate_ref[...], res_ref[...]
    toks = u_ref.shape[0]
    blocks = toks // SUB
    lag = (2 * SUB - lax.broadcasted_iota(jnp.int32, (rows, 2 * SUB), 1)) % (2 * SUB)
    terms = jnp.where(lag < SUB, res * jnp.exp(-rate * lag.astype(F32)), 0.0)
    wheel = jnp.sum(terms.reshape(groups, modes, 2 * SUB), axis=1)
    half = SUB // 2
    for g in range(groups):
        base = jnp.broadcast_to(wheel[g : g + 1], (8, 2 * SUB))
        base = pltpu.roll(base, 0, 1, stride=1, stride_axis=0)
        low = jnp.concatenate(
            [pltpu.roll(base, half + 8 * i, 1)[:, :SUB] for i in range(half // 8)], axis=0
        ).astype(BF16)
        taps_ref[g, half:, :] = low
        taps_ref[g, :half, :half] = low[:, half:]
        taps_ref[g, :half, half:] = jnp.zeros((half, half), BF16)

    mask = own_mask(rows, TILE, modes, width)
    left = (SUB - 1) - lax.broadcasted_iota(jnp.int32, (rows, SUB), 1)
    inject = jnp.exp(-rate * left.astype(F32)).astype(BF16)
    after = lax.broadcasted_iota(jnp.int32, (SUB, rows), 0) + 1
    readout = (
        res_row_ref[...] * jnp.exp(-rate_row_ref[...] * after.astype(F32))
    ).astype(BF16)
    decay = jnp.exp(-rate * SUB)
    state = None
    lane_group = (lax.broadcasted_iota(jnp.int32, (SUB, 2 * TILE), 1) % TILE) // width
    for pair in range(0, blocks, 2):
        cuts = [u_ref[(pair + i) * SUB : (pair + i + 1) * SUB, :] for i in range(2)]
        both = jnp.concatenate(cuts, axis=1)
        z = dot32(taps_ref[0], both)
        for g in range(1, groups):
            z = jnp.where(lane_group == g, dot32(taps_ref[g], both), z)
        sums = dot32(inject, both)
        for i in range(2):
            n = pair + i
            out = z[:, i * TILE : (i + 1) * TILE]
            if state is not None:
                out = out + dot32(readout, state.astype(BF16))
            z_ref[n * SUB : (n + 1) * SUB, :] = out
            own = jnp.where(mask, sums[:, i * TILE : (i + 1) * TILE], 0.0)
            state = own if state is None else decay * state + own


def local_conv(u, rate_col, res_col, rate_row, res_row, modes, width):
    toks, chans = u.shape
    rows = TILE // width * modes
    col = pl.BlockSpec((rows, 1), lambda i: (i, 0))
    row = pl.BlockSpec((1, rows), lambda i: (0, i))
    feat = pl.BlockSpec((toks, TILE), lambda i: (0, i))
    return pl.pallas_call(
        functools.partial(local_kernel, modes, width),
        grid=(chans // TILE,),
        in_specs=[feat, col, col, row, row],
        out_specs=feat,
        out_shape=jax.ShapeDtypeStruct((toks, chans), F32),
        scratch_shapes=[pltpu.VMEM((TILE // width, SUB, SUB), BF16)],
        compiler_params=pltpu.CompilerParams(vmem_limit_bytes=24 << 20),
        name="local_conv",
    )(u, rate_col, res_col, rate_row, res_row)


def gate_kernel(
    modes, width, toks, place_ref, lag_ref, z_ref, q_ref, rate_row_ref, res_row_ref,
    rate_ref, *refs
):
    y_ref, states = refs[-1], refs[:-1]
    rate = rate_ref[...]
    entering = jnp.zeros(rate.shape, F32)
    at = 0
    for piece in states:
        for j in range(piece.shape[0]):
            lag = lag_ref[at]
            span = (jnp.maximum(lag, 0) * toks).astype(F32)
            weight = jnp.where(lag >= 0, jnp.exp(-rate * span), 0.0)
            entering = entering + weight * piece[j].astype(F32)
            at += 1
    first = place_ref[0] * SUB + 1
    rows = TILE // width * modes
    mask = own_mask(rows, TILE, modes, width)
    for tile in range(q_ref.shape[1] // TILE):
        lanes = slice(tile * TILE, (tile + 1) * TILE)
        group = slice(tile * rows, (tile + 1) * rows)
        after = lax.broadcasted_iota(jnp.int32, (SUB, rows), 0) + first
        readout = (
            res_row_ref[:, group] * jnp.exp(-rate_row_ref[:, group] * after.astype(F32))
        ).astype(BF16)
        spread = jnp.concatenate([entering[:, lanes]] * (TILE // width), axis=0)
        spread = jnp.where(mask, spread, 0.0).astype(BF16)
        z = z_ref[:, lanes] + dot32(readout, spread)
        y_ref[:, lanes] = (q_ref[:, lanes].astype(F32) * z).astype(BF16)


def gate(place, lags, z, query_feat, rate_row, res_row, rate_mc, states, modes, width):
    toks, chans = query_feat.shape
    whole = lambda a: pl.BlockSpec(a.shape, lambda i, p, g: (0,) * a.ndim)
    block = pl.BlockSpec((SUB, chans), lambda i, p, g: (p[0], 0))
    return pl.pallas_call(
        functools.partial(gate_kernel, modes, width, toks),
        grid_spec=pltpu.PrefetchScalarGridSpec(
            num_scalar_prefetch=2,
            grid=(1,),
            in_specs=[block, block, whole(rate_row), whole(res_row), whole(rate_mc)]
            + [whole(s) for s in states],
            out_specs=pl.BlockSpec((SUB, chans), lambda i, p, g: (0, 0)),
        ),
        out_shape=jax.ShapeDtypeStruct((SUB, chans), BF16),
        compiler_params=pltpu.CompilerParams(vmem_limit_bytes=24 << 20),
        name="gate",
    )(place, lags, z, query_feat, rate_row, res_row, rate_mc, *states)


def share_kernel(ya_ref, yb_ref, *refs):
    out_ref, weights = refs[-1], refs[:-1]
    half = len(weights) // 2
    at = 0
    for wa, wb in zip(weights[:half], weights[half:]):
        cols = wa.shape[1]
        total = dot32(ya_ref[...], wa[...]) + dot32(yb_ref[...], wb[...])
        out_ref[:, at : at + cols] = total.astype(BF16)
        at += cols


def share(ya, yb, near, far):
    cols = sum(w.shape[1] for w in near)
    return pl.pallas_call(
        share_kernel,
        out_shape=jax.ShapeDtypeStruct((ya.shape[0], cols), BF16),
        compiler_params=pltpu.CompilerParams(vmem_limit_bytes=32 << 20),
        cost_estimate=pl.CostEstimate(
            flops=4 * ya.size * cols, bytes_accessed=4 * ya.shape[1] * cols, transcendentals=0
        ),
        name="share",
    )(ya, yb, *near, *far)


def finish_kernel(count, place_ref, ya_ref, yb_ref, got_ref, *refs):
    out_ref = refs[-1]
    weights = refs[: 2 * count]
    at = 0
    for wa, wb in zip(weights[:count], weights[count:]):
        cols = wa.shape[1]
        total = dot32(ya_ref[...], wa[...]) + dot32(yb_ref[...], wb[...])
        total = total + got_ref[:, at : at + cols].astype(F32)
        out_ref[:, at : at + cols] = total.astype(BF16)
        at += cols


def finish(place, ya, yb, got, near, far, out, all_cols):
    rows, cols = got.shape
    whole = lambda a: pl.BlockSpec(a.shape, lambda i, p: (0,) * a.ndim)
    args = [ya, yb, got, *near, *far]
    specs = [whole(a) for a in args]
    alias = {}
    if out is not None:
        alias = {1 + len(args): 0}
        args.append(out)
        specs.append(pl.BlockSpec(memory_space=pl.ANY))
    return pl.pallas_call(
        functools.partial(finish_kernel, len(near)),
        grid_spec=pltpu.PrefetchScalarGridSpec(
            num_scalar_prefetch=1,
            grid=(1,),
            in_specs=specs,
            out_specs=pl.BlockSpec((rows, cols), lambda i, p: (0, p[0])),
        ),
        out_shape=jax.ShapeDtypeStruct((rows, all_cols), BF16),
        input_output_aliases=alias,
        compiler_params=pltpu.CompilerParams(vmem_limit_bytes=32 << 20),
        cost_estimate=pl.CostEstimate(
            flops=4 * ya.size * cols, bytes_accessed=4 * ya.shape[1] * cols, transcendentals=0
        ),
        name="finish",
    )(place, *args)


def flip(x, axis, size, bits):
    return lax.ppermute(x, axis, [(i, i ^ bits) for i in range(size)])


def spread(halves, size):
    left, right = halves
    across = [flip(w, "seq", size, 2) for w in halves]
    along = [flip(w, "seq", size, 4) for w in halves]
    corner = [flip(across[0], "seq", size, 4), flip(along[1], "seq", size, 2)]
    pieces = {0: halves, 2: across, 4: along, 6: corner}
    for m in (0, 2, 4, 6):
        pieces[m + 1] = [flip(w, "seq", size, 1) for w in pieces[m]]
    return pieces


def on_device(seq_size, ch_size, query_feat, key_feat, value_feat, decay_rates, residues, out_weight):
    toks, chans = query_feat.shape
    groups, modes = decay_rates.shape
    width = chans // groups
    piece_cols = out_weight.shape[1]
    all_cols = piece_cols * seq_size
    me = lax.axis_index("seq").astype(jnp.int32)
    plane = lax.axis_index("ch").astype(jnp.int32)

    if seq_size == 8:
        mid = piece_cols // 2
        halves = [out_weight[:, :mid], out_weight[:, mid:]]
        far_halves = [flip(w, "ch", ch_size, 2) for w in halves]
        near, far = spread(halves, seq_size), spread(far_halves, seq_size)
        order = [(near[m], far[m], me ^ m) for m in range(8)]
    else:
        gather = lambda w: lax.all_gather(w, "seq", axis=1, tiled=True)
        near, far = gather(out_weight), gather(flip(out_weight, "ch", ch_size, 2))
        order = [([near], [far], jnp.int32(0))]

    rate_col = decay_rates.reshape(groups * modes, 1)
    res_col = residues.reshape(groups * modes, 1)
    rate_row = decay_rates.reshape(1, groups * modes)
    res_row = residues.reshape(1, groups * modes)
    rate_mc = jnp.repeat(decay_rates.T, width, axis=1)

    u, final_state = range_state(key_feat, value_feat, rate_col, modes, width)
    final_state = final_state[None]
    if seq_size == 8:
        states = [final_state] + [flip(final_state, "seq", seq_size, m) for m in range(1, 8)]
        origin = me ^ jnp.arange(8, dtype=jnp.int32)
    else:
        states = [lax.all_gather(final_state, "seq", axis=0, tiled=True)]
        origin = jnp.arange(seq_size, dtype=jnp.int32)
    lags = me - 1 - origin
    z = local_conv(u, rate_col, res_col, rate_row, res_row, modes, width)

    def gated(slot):
        place = (plane ^ slot).reshape(1)
        return gate(place, lags, z, query_feat, rate_row, res_row, rate_mc, states, modes, width)

    far_other = flip(gated(3), "ch", ch_size, 2)
    far_own = flip(gated(2), "ch", ch_size, 2)
    near_other, near_own = gated(1), gated(0)

    got = [flip(share(near_other, far_other, a, b), "ch", ch_size, 1) for a, b, _ in order]
    out = None
    for (a, b, place), part in zip(order, got):
        out = finish(place.reshape(1), near_own, far_own, part, a, b, out, all_cols)
    return out


def solution(mesh):
    in_specs = (
        P("seq", "ch"),
        P("seq", "ch"),
        P("seq", "ch"),
        P("ch", None),
        P("ch", None),
        P("ch", "seq"),
    )
    out_specs = P(("seq", "ch"), None)
    body = functools.partial(on_device, mesh.shape["seq"], mesh.shape["ch"])
    return jax.shard_map(
        body, mesh=mesh, in_specs=in_specs, out_specs=out_specs, check_vma=False
    )
```

```python
import functools

import jax
import jax.numpy as jnp
from jax import lax
from jax.experimental import pallas as pl
from jax.experimental.pallas import tpu as pltpu
from jax.sharding import PartitionSpec as P

SUB = 256
TILE = 128
F32 = jnp.float32
BF16 = jnp.bfloat16


def dot32(a, b):
    return jnp.dot(a, b, preferred_element_type=F32)


def own_mask(rows, cols, modes, width):
    r = lax.broadcasted_iota(jnp.int32, (rows, cols), 0) // modes
    c = lax.broadcasted_iota(jnp.int32, (rows, cols), 1) // width
    return r == c


def as_column(table, first, count):
    modes, groups = table.shape
    rows = jnp.broadcast_to(table[None], (count, modes, groups)).reshape(count * modes, groups)
    group = lax.broadcasted_iota(jnp.int32, rows.shape, 0) // modes + first
    pick = group == lax.broadcasted_iota(jnp.int32, rows.shape, 1)
    return jnp.sum(jnp.where(pick, rows, 0.0), axis=1, keepdims=True)


def as_row(column):
    size = column.shape[0]
    same = lax.broadcasted_iota(jnp.int32, (size, size), 0)
    same = same == lax.broadcasted_iota(jnp.int32, (size, size), 1)
    return jnp.sum(jnp.where(same, column, 0.0), axis=0, keepdims=True)


VMEM_BYTES = 56 << 20
SHORT = pl.CostEstimate(flops=1, bytes_accessed=1, transcendentals=0)
LONG = pl.CostEstimate(flops=1 << 36, bytes_accessed=1 << 28, transcendentals=0)


def range_state_kernel(width, me_ref, k_ref, v_ref, rate_ref, u_ref, f_ref):
    u = (k_ref[...].astype(F32) * v_ref[...].astype(F32)).astype(BF16)
    u_ref[...] = u
    toks, cols = u.shape
    modes = rate_ref.shape[0]
    count = cols // width
    rate = as_column(rate_ref[...], pl.program_id(0) * count, count)
    rows = rate.shape[0]
    left = (SUB - 1) - lax.broadcasted_iota(jnp.int32, (rows, SUB), 1)
    inject = jnp.exp(-rate * left.astype(F32)).astype(BF16)
    decay = jnp.exp(-rate * SUB)
    sums = dot32(inject, u[:SUB])
    for n in range(1, toks // SUB):
        sums = decay * sums + dot32(inject, u[n * SUB : (n + 1) * SUB])
    sums = jnp.where(own_mask(rows, cols, modes, width), sums, 0.0)
    for to in range(f_ref.shape[0]):
        lag = to - 1 - me_ref[0]
        weight = jnp.exp(-rate * (jnp.maximum(lag, 0) * toks).astype(F32))
        there = (weight * sums).reshape(rows // modes, modes, cols)
        f_ref[to] = jnp.where(lag >= 0, jnp.sum(there, axis=0), 0.0).astype(BF16)


def range_state(me, key_feat, value_feat, rates, seq_size, width):
    toks, chans = key_feat.shape
    modes = rates.shape[0]
    step = 256
    feat = pl.BlockSpec((toks, step), lambda i, p: (0, i))
    return pl.pallas_call(
        functools.partial(range_state_kernel, width),
        grid_spec=pltpu.PrefetchScalarGridSpec(
            num_scalar_prefetch=1,
            grid=(chans // step,),
            in_specs=[feat, feat, pl.BlockSpec(rates.shape, lambda i, p: (0, 0))],
            out_specs=[feat, pl.BlockSpec((seq_size, modes, step), lambda i, p: (0, 0, i))],
        ),
        out_shape=[
            jax.ShapeDtypeStruct((toks, chans), BF16),
            jax.ShapeDtypeStruct((seq_size, modes, chans), BF16),
        ],
        compiler_params=pltpu.CompilerParams(vmem_limit_bytes=VMEM_BYTES),
        cost_estimate=SHORT,
        name="range_state",
    )(me, key_feat, value_feat, rates)


def local_kernel(width, u_ref, rate_ref, res_ref, z_ref, rows_ref, taps_ref, split_ref):
    modes, groups = rate_ref.shape[0], TILE // width
    rows = groups * modes
    rate, res = (as_column(r[...], pl.program_id(0) * groups, groups) for r in (rate_ref, res_ref))
    rate_row, res_row = as_row(rate), as_row(res)
    rows_ref[0:1, :] = rate_row
    rows_ref[1:2, :] = res_row
    blocks = u_ref.shape[0] // SUB
    lag = 2 * SUB - lax.broadcasted_iota(jnp.int32, (rows, 2 * SUB), 1)
    lag = jnp.where(lag == 2 * SUB, 0, lag)
    terms = jnp.where(lag < SUB, res * jnp.exp(-rate * lag.astype(F32)), 0.0)
    wheel = jnp.sum(terms.reshape(groups, modes, 2 * SUB), axis=1)
    half = SUB // 2
    both = jnp.concatenate([u_ref[n * SUB : (n + 1) * SUB, :] for n in range(blocks)], axis=1)
    lane_group = (lax.broadcasted_iota(jnp.int32, (1, blocks * TILE), 1) % TILE) // width
    for g in range(groups):
        base = jnp.broadcast_to(wheel[g : g + 1], (half, 2 * SUB))
        low = pltpu.roll(base, half, 1, stride=1, stride_axis=0)[:, :SUB].astype(BF16)
        taps_ref[half:, g * SUB : (g + 1) * SUB] = low
        taps_ref[:half, g * SUB : g * SUB + half] = low[:, half:]
        taps_ref[:half, g * SUB + half : (g + 1) * SUB] = jnp.zeros((half, half), BF16)
        split_ref[g * SUB : (g + 1) * SUB, :] = both * (lane_group == g).astype(BF16)

    mask = own_mask(rows, TILE, modes, width)
    left = (SUB - 1) - lax.broadcasted_iota(jnp.int32, (rows, SUB), 1)
    inject = jnp.exp(-rate * left.astype(F32)).astype(BF16)
    sums = dot32(inject, both[:, : (blocks - 1) * TILE])
    decay = jnp.exp(-rate * SUB)
    state, starts = jnp.zeros((rows, TILE), F32), []
    for n in range(blocks - 1):
        own = jnp.where(mask, sums[:, n * TILE : (n + 1) * TILE], 0.0)
        state = decay * state + own
        starts.append(state.astype(BF16))
    after = lax.broadcasted_iota(jnp.int32, (SUB, rows), 0) + 1
    readout = (res_row * jnp.exp(-rate_row * after.astype(F32))).astype(BF16)
    carried = dot32(readout, jnp.concatenate(starts, axis=1))
    z = dot32(taps_ref[...], split_ref[...])
    z_ref[:SUB, :] = z[:, :TILE]
    for n in range(1, blocks):
        z_ref[n * SUB : (n + 1) * SUB, :] = (
            z[:, n * TILE : (n + 1) * TILE] + carried[:, (n - 1) * TILE : n * TILE]
        )


def local_conv(u, rates, residues, width):
    toks, chans = u.shape
    modes = rates.shape[0]
    groups = TILE // width
    rows = groups * modes
    table = pl.BlockSpec(rates.shape, lambda i: (0, 0))
    feat = pl.BlockSpec((toks, TILE), lambda i: (0, i))
    return pl.pallas_call(
        functools.partial(local_kernel, width),
        grid=(chans // TILE,),
        in_specs=[feat, table, table],
        out_specs=[feat, pl.BlockSpec((2, rows), lambda i: (0, i))],
        out_shape=[
            jax.ShapeDtypeStruct((toks, chans), F32),
            jax.ShapeDtypeStruct((2, rates.size), F32),
        ],
        scratch_shapes=[
            pltpu.VMEM((SUB, groups * SUB), BF16),
            pltpu.VMEM((groups * SUB, toks // SUB * TILE), BF16),
        ],
        compiler_params=pltpu.CompilerParams(vmem_limit_bytes=VMEM_BYTES),
        cost_estimate=SHORT,
        name="local_conv",
    )(u, rates, residues)


def gate_kernel(modes, width, counts, place_ref, z_ref, q_ref, rows_ref, state_ref, *y_refs):
    y_refs = list(zip(y_refs, counts))
    step = pl.program_id(0)
    entering = jnp.sum(state_ref[...].astype(F32), axis=0)
    first = place_ref[step] * SUB + 1
    rows = TILE // width * modes
    mask = own_mask(rows, TILE, modes, width)
    tiles = []
    for tile in range(q_ref.shape[1] // TILE):
        lanes = slice(tile * TILE, (tile + 1) * TILE)
        group = slice(tile * rows, (tile + 1) * rows)
        after = lax.broadcasted_iota(jnp.int32, (SUB, rows), 0) + first
        readout = (
            rows_ref[1:2, group] * jnp.exp(-rows_ref[0:1, group] * after.astype(F32))
        ).astype(BF16)
        spread = jnp.concatenate([entering[:, lanes]] * (TILE // width), axis=0)
        spread = jnp.where(mask, spread, 0.0).astype(BF16)
        z = z_ref[:, lanes] + dot32(readout, spread)
        tiles.append((q_ref[:, lanes].astype(F32) * z).astype(BF16))
    at = 0
    for y_ref, count in y_refs:

        @pl.when((step >= at) & (step < at + count))
        def _():
            y_ref[...] = jnp.concatenate(tiles, axis=1)

        at += count


def gate(places, counts, z, query_feat, rows, states, width):
    modes, chans = states.shape[1], query_feat.shape[1]
    whole = lambda a: pl.BlockSpec(a.shape, lambda i, p: (0,) * a.ndim)
    block = pl.BlockSpec((SUB, chans), lambda i, p: (p[i], 0))

    def result(first, count):
        return pl.BlockSpec((SUB, chans), lambda i, p: (jnp.clip(i - first, 0, count - 1), 0))

    return pl.pallas_call(
        functools.partial(gate_kernel, modes, width, counts),
        grid_spec=pltpu.PrefetchScalarGridSpec(
            num_scalar_prefetch=1,
            grid=(sum(counts),),
            in_specs=[block, block, whole(rows), whole(states)],
            out_specs=[result(sum(counts[:n]), count) for n, count in enumerate(counts)],
        ),
        out_shape=[jax.ShapeDtypeStruct((n * SUB, chans), BF16) for n in counts],
        compiler_params=pltpu.CompilerParams(vmem_limit_bytes=VMEM_BYTES),
        cost_estimate=SHORT,
        name="gate",
    )(places, z, query_feat, rows, states)


def share_kernel(sets, count, added, *refs):
    near = jnp.concatenate([r[...] for r in refs[:sets]], axis=0)
    far = jnp.concatenate([r[...] for r in refs[sets : 2 * sets]], axis=0)
    weights, outs = refs[2 * sets : 2 * sets + 2 * count], refs[2 * sets + 2 * count + added :]
    rows = near.shape[0] // len(outs)
    at = 0
    for wn, wf in zip(weights[:count], weights[count:]):
        cols = wn.shape[1]
        total = dot32(near, wn[...]) + dot32(far, wf[...])
        if added:
            total = total + refs[-len(outs) - 1][:, at : at + cols].astype(F32)
        total = total.astype(BF16)
        for i, out in enumerate(outs):
            out[:, at : at + cols] = total[i * rows : (i + 1) * rows]
        at += cols


def share(near, far, near_w, far_w, cols, parts=1, add=None, cost=SHORT):
    depth = near[0][0].shape[1]
    rows = lambda n: pl.BlockSpec((SUB, depth), lambda i: (n, 0))
    part = lambda col: pl.BlockSpec((depth, cols), lambda i: (0, col))
    whole = lambda *shape: pl.BlockSpec(shape, lambda i: (0, 0))
    height, total = len(near) * SUB, cols * len(near_w)
    extra = [] if add is None else [add]
    return pl.pallas_call(
        functools.partial(share_kernel, len(near), len(near_w), len(extra)),
        grid=(1,),
        in_specs=[rows(n) for _, n in near + far]
        + [part(col) for _, col in near_w + far_w]
        + [whole(*e.shape) for e in extra],
        out_specs=[whole(height // parts, total)] * parts,
        out_shape=[jax.ShapeDtypeStruct((height // parts, total), BF16)] * parts,
        compiler_params=pltpu.CompilerParams(vmem_limit_bytes=VMEM_BYTES),
        cost_estimate=cost,
        name="share",
    )(*[a for a, _ in near + far + near_w + far_w], *extra)


def place_kernel(spots, place_ref, *refs):
    out_ref, total_ref, sem = refs[-3:]
    cols = total_ref.shape[2]
    copies = []
    for j, spot in enumerate(spots):
        terms = [refs[i][:, n * cols : (n + 1) * cols] for i, n in spot]
        total = terms[0] if len(terms) == 1 else sum(t.astype(F32) for t in terms).astype(BF16)
        total_ref[j] = total
        to = pl.ds(pl.multiple_of(place_ref[j] * cols, cols), cols)
        copies.append(pltpu.make_async_copy(total_ref.at[j], out_ref.at[:, to], sem.at[j]))
        copies[-1].start()
    for copy in copies:
        copy.wait()


def place(places, terms, cols, out, all_cols, cost, awaited=()):
    arrays, spots = [], []
    for group in terms:
        spot = []
        for array, n in group:
            known = [i for i, a in enumerate(arrays) if a is array]
            if not known:
                known = [len(arrays)]
                arrays.append(array)
            spot.append((known[0], n))
        spots.append(spot)
    rows = arrays[0].shape[0]
    specs = [pl.BlockSpec(a.shape, lambda i, p: (0, 0)) for a in arrays]
    alias = {}
    arrays += awaited
    specs += [pl.BlockSpec(memory_space=pl.ANY)] * len(awaited)
    if out is not None:
        alias = {1 + len(arrays): 0}
        arrays.append(out)
        specs.append(pl.BlockSpec(memory_space=pl.ANY))
    return pl.pallas_call(
        functools.partial(place_kernel, spots),
        grid_spec=pltpu.PrefetchScalarGridSpec(
            num_scalar_prefetch=1,
            grid=(1,),
            in_specs=specs,
            out_specs=pl.BlockSpec(memory_space=pl.ANY),
            scratch_shapes=[
                pltpu.VMEM((len(spots), rows, cols), BF16),
                pltpu.SemaphoreType.DMA((len(spots),)),
            ],
        ),
        out_shape=jax.ShapeDtypeStruct((rows, all_cols), BF16),
        input_output_aliases=alias,
        compiler_params=pltpu.CompilerParams(vmem_limit_bytes=VMEM_BYTES),
        cost_estimate=cost,
        name="place",
    )(places, *arrays)


def flip(x, axis, size, bits):
    return lax.ppermute(x, axis, [(i, i ^ bits) for i in range(size)])


def after(x, *others):
    return lax.optimization_barrier((x, *others))[0]


def on_device(seq_size, ch_size, query_feat, key_feat, value_feat, decay_rates, residues, out_weight):
    toks, chans = query_feat.shape
    groups, modes = decay_rates.shape
    width = chans // groups
    piece_cols = out_weight.shape[1]
    all_cols = piece_cols * seq_size
    me = lax.axis_index("seq").astype(jnp.int32)
    plane = lax.axis_index("ch").astype(jnp.int32)
    far_plane = lambda x: flip(x, "ch", ch_size, 2)
    next_plane = lambda x: flip(x, "ch", ch_size, 1)

    rates, residues = decay_rates.T, residues.T
    u, ends = range_state(me.reshape(1), key_feat, value_feat, rates, seq_size, width)
    states = lax.all_to_all(ends, "seq", 0, 0, tiled=True)
    z, rows = local_conv(u, rates, residues, width)

    def gated(slots, counts, *hold):
        places = plane ^ jnp.array(slots, jnp.int32)
        return gate(places, counts, after(z, *hold), query_feat, rows, states, width)

    if seq_size != 8:
        y_3, near, y_2 = gated((3, 1, 0, 2), (1, 2, 1))
        near_w = lax.all_gather(out_weight, "seq", axis=1, tiled=True)
        far_w = lax.all_gather(far_plane(out_weight), "seq", axis=1, tiled=True)
        far_other, far_own = far_plane(y_3), far_plane(y_2)
        near_w, far_w = [(near_w, 0)], [(far_w, 0)]
        (part,) = share([(near, 0)], [(far_other, 0)], near_w, far_w, all_cols)
        (own,) = share([(near, 1)], [(far_own, 0)], near_w, far_w, all_cols)
        return (own.astype(F32) + next_plane(part).astype(F32)).astype(BF16)

    core = lambda x: flip(x, "seq", seq_size, 1)
    pairs = [(s * ch_size + c, (s ^ 1) * ch_size + (c ^ 1)) for s in range(seq_size) for c in range(ch_size)]
    next_cross = lambda x: lax.ppermute(x, ("seq", "ch"), pairs)
    across = lambda x: flip(x, "seq", seq_size, 2)
    along = lambda x: flip(x, "seq", seq_size, 4)

    half = piece_cols // 2
    first, second = slice(0, half), slice(half, None)

    n_a = out_weight[:, first]
    f_a = far_plane(n_a)
    n_x, n_y = across(out_weight), along(out_weight)
    (y_3,) = gated((3,), (1,), n_x, n_y)

    y_far_other = far_plane(y_3)
    f_a = after(f_a, y_3)
    f_ax, f_ay = across(f_a), along(f_a)
    n_ac = along(after(n_x, f_a)[:, first])
    near, y_2 = gated((1, 0, 2), (2, 1), n_x, n_y, f_a)
    near_sib = core(near)
    n_b = after(out_weight, near)[:, second]
    y_far_other, f_ax, f_ay, n_ac, n_b = lax.optimization_barrier(
        (y_far_other, f_ax, f_ay, n_ac, n_b)
    )

    f_b = far_plane(n_b)
    far_other_sib = core(y_far_other)
    f_ac = along(after(f_ax, far_other_sib))
    n_bc = across(after(n_y, near_sib, far_other_sib)[:, second])
    near_w = [(out_weight, 0), (n_x, 0), (n_y, 0), (n_ac, 0)]
    near_w += [(out_weight, 1), (n_x, 1), (n_y, 1), (n_bc, 0)]
    far_w = [(f_a, 0), (f_ax, 0), (f_ay, 0)]
    near_other, near_own = [(near, 0), (near_sib, 0)], [(near, 1), (near_sib, 1)]
    far_other = [(y_far_other, 0), (far_other_sib, 0)]

    def products(near, far, pieces, **kw):
        return share(near, far, [near_w[i] for i in pieces], [far_w[i] for i in pieces], half, **kw)

    (ready_1,) = products(near_other, far_other, range(2))
    part_1 = next_plane(ready_1)

    f_b, f_ac, n_bc = lax.optimization_barrier((f_b, f_ac, n_bc))
    near_w[7] = (n_bc, 0)
    y_far_own = far_plane(after(y_2, f_b))
    f_bx, f_by, f_bc = across(f_b), along(f_b), flip(f_b, "seq", seq_size, 6)
    far_w += [(f_ac, 0), (f_b, 0)]
    (ready_2,) = products(near_other, far_other, range(2, 5))
    part_2 = next_plane(after(ready_2, part_1))
    far_w += [(after(f_bx, y_far_own), 0), (f_by, 0), (f_bc, 0)]
    mine, other = products(near_other, far_other, range(5, 8), parts=2, cost=LONG)
    part_3 = next_plane(mine), next_cross(other)

    far_own_sib = core(after(y_far_own, mine))
    far_own = [(y_far_own, 0), (far_own_sib, 0)]
    own, cross = [], []
    for pieces, part in ((range(2), part_1), (range(2, 5), part_2), (range(5, 8), None)):
        mine, other = products(near_own, far_own, pieces, parts=2, add=part)
        other = core(other)
        own += [[(mine, n)] for n in range(len(pieces))]
        cross += [[(other, n)] for n in range(len(pieces))]
    for n in range(3):
        own[5 + n].append((part_3[0], n))
        cross[5 + n].append((part_3[1], n))
    spots = lambda s: jnp.stack([(me ^ s ^ (i % 4 * 2)) * 2 + i // 4 for i in range(8)])
    out = place(spots(0), own, half, None, all_cols, LONG, part_3[1:])
    return place(spots(1), cross, half, out, all_cols, SHORT)


def solution(mesh):
    in_specs = (
        P("seq", "ch"),
        P("seq", "ch"),
        P("seq", "ch"),
        P("ch", None),
        P("ch", None),
        P("ch", "seq"),
    )
    out_specs = P(("seq", "ch"), None)
    body = functools.partial(on_device, mesh.shape["seq"], mesh.shape["ch"])
    return jax.shard_map(
        body, mesh=mesh, in_specs=in_specs, out_specs=out_specs, check_vma=False
    )
```

```python
import functools

import jax
import jax.numpy as jnp
from jax import lax
from jax.experimental import pallas as pl
from jax.experimental.pallas import tpu as pltpu
from jax.sharding import PartitionSpec as P

SUB = 256
TILE = 128
F32 = jnp.float32
BF16 = jnp.bfloat16


def dot32(a, b):
    return jnp.dot(a, b, preferred_element_type=F32)


def own_mask(rows, cols, modes, width):
    r = lax.broadcasted_iota(jnp.int32, (rows, cols), 0) // modes
    c = lax.broadcasted_iota(jnp.int32, (rows, cols), 1) // width
    return r == c


def as_column(table, first, count):
    modes, groups = table.shape
    rows = jnp.broadcast_to(table[None], (count, modes, groups)).reshape(count * modes, groups)
    group = lax.broadcasted_iota(jnp.int32, rows.shape, 0) // modes + first
    pick = group == lax.broadcasted_iota(jnp.int32, rows.shape, 1)
    return jnp.sum(jnp.where(pick, rows, 0.0), axis=1, keepdims=True)


def as_row(column):
    size = column.shape[0]
    same = lax.broadcasted_iota(jnp.int32, (size, size), 0)
    same = same == lax.broadcasted_iota(jnp.int32, (size, size), 1)
    return jnp.sum(jnp.where(same, column, 0.0), axis=0, keepdims=True)


VMEM_BYTES = 56 << 20
SHORT = pl.CostEstimate(flops=1, bytes_accessed=1, transcendentals=0)
LONG = pl.CostEstimate(flops=1 << 36, bytes_accessed=1 << 28, transcendentals=0)


def range_state_kernel(width, me_ref, k_ref, v_ref, rate_ref, u_ref, f_ref):
    u = (k_ref[...].astype(F32) * v_ref[...].astype(F32)).astype(BF16)
    u_ref[...] = u
    toks, cols = u.shape
    modes = rate_ref.shape[0]
    count = cols // width
    rate = as_column(rate_ref[...], pl.program_id(0) * count, count)
    rows = rate.shape[0]
    left = (SUB - 1) - lax.broadcasted_iota(jnp.int32, (rows, SUB), 1)
    inject = jnp.exp(-rate * left.astype(F32)).astype(BF16)
    decay = jnp.exp(-rate * SUB)
    sums = dot32(inject, u[:SUB])
    for n in range(1, toks // SUB):
        sums = decay * sums + dot32(inject, u[n * SUB : (n + 1) * SUB])
    sums = jnp.where(own_mask(rows, cols, modes, width), sums, 0.0)
    for to in range(f_ref.shape[0]):
        lag = to - 1 - me_ref[0]
        weight = jnp.exp(-rate * (jnp.maximum(lag, 0) * toks).astype(F32))
        there = (weight * sums).reshape(rows // modes, modes, cols)
        f_ref[to] = jnp.where(lag >= 0, jnp.sum(there, axis=0), 0.0).astype(BF16)


def range_state(me, key_feat, value_feat, rates, seq_size, width):
    toks, chans = key_feat.shape
    modes = rates.shape[0]
    step = 256
    feat = pl.BlockSpec((toks, step), lambda i, p: (0, i))
    return pl.pallas_call(
        functools.partial(range_state_kernel, width),
        grid_spec=pltpu.PrefetchScalarGridSpec(
            num_scalar_prefetch=1,
            grid=(chans // step,),
            in_specs=[feat, feat, pl.BlockSpec(rates.shape, lambda i, p: (0, 0))],
            out_specs=[feat, pl.BlockSpec((seq_size, modes, step), lambda i, p: (0, 0, i))],
        ),
        out_shape=[
            jax.ShapeDtypeStruct((toks, chans), BF16),
            jax.ShapeDtypeStruct((seq_size, modes, chans), BF16),
        ],
        compiler_params=pltpu.CompilerParams(vmem_limit_bytes=VMEM_BYTES),
        cost_estimate=SHORT,
        name="range_state",
    )(me, key_feat, value_feat, rates)


def local_kernel(width, u_ref, rate_ref, res_ref, z_ref, rows_ref, taps_ref, split_ref):
    modes, groups = rate_ref.shape[0], TILE // width
    rows = groups * modes
    rate, res = (as_column(r[...], pl.program_id(0) * groups, groups) for r in (rate_ref, res_ref))
    rate_row, res_row = as_row(rate), as_row(res)
    rows_ref[0:1, :] = rate_row
    rows_ref[1:2, :] = res_row
    blocks = u_ref.shape[0] // SUB
    lag = 2 * SUB - lax.broadcasted_iota(jnp.int32, (rows, 2 * SUB), 1)
    lag = jnp.where(lag == 2 * SUB, 0, lag)
    terms = jnp.where(lag < SUB, res * jnp.exp(-rate * lag.astype(F32)), 0.0)
    wheel = jnp.sum(terms.reshape(groups, modes, 2 * SUB), axis=1)
    half = SUB // 2
    both = jnp.concatenate([u_ref[n * SUB : (n + 1) * SUB, :] for n in range(blocks)], axis=1)
    lane_group = (lax.broadcasted_iota(jnp.int32, (1, blocks * TILE), 1) % TILE) // width
    for g in range(groups):
        base = jnp.broadcast_to(wheel[g : g + 1], (half, 2 * SUB))
        low = pltpu.roll(base, half, 1, stride=1, stride_axis=0)[:, :SUB].astype(BF16)
        taps_ref[half:, g * SUB : (g + 1) * SUB] = low
        taps_ref[:half, g * SUB : g * SUB + half] = low[:, half:]
        taps_ref[:half, g * SUB + half : (g + 1) * SUB] = jnp.zeros((half, half), BF16)
        split_ref[g * SUB : (g + 1) * SUB, :] = both * (lane_group == g).astype(BF16)

    mask = own_mask(rows, TILE, modes, width)
    left = (SUB - 1) - lax.broadcasted_iota(jnp.int32, (rows, SUB), 1)
    inject = jnp.exp(-rate * left.astype(F32)).astype(BF16)
    sums = dot32(inject, both[:, : (blocks - 1) * TILE])
    decay = jnp.exp(-rate * SUB)
    state, starts = jnp.zeros((rows, TILE), F32), []
    for n in range(blocks - 1):
        own = jnp.where(mask, sums[:, n * TILE : (n + 1) * TILE], 0.0)
        state = decay * state + own
        starts.append(state.astype(BF16))
    after = lax.broadcasted_iota(jnp.int32, (SUB, rows), 0) + 1
    readout = (res_row * jnp.exp(-rate_row * after.astype(F32))).astype(BF16)
    carried = dot32(readout, jnp.concatenate(starts, axis=1))
    z = dot32(taps_ref[...], split_ref[...])
    z_ref[:SUB, :] = z[:, :TILE].astype(BF16)
    for n in range(1, blocks):
        z_ref[n * SUB : (n + 1) * SUB, :] = (
            z[:, n * TILE : (n + 1) * TILE] + carried[:, (n - 1) * TILE : n * TILE]
        ).astype(BF16)


def local_conv(u, rates, residues, width):
    toks, chans = u.shape
    modes = rates.shape[0]
    groups = TILE // width
    rows = groups * modes
    table = pl.BlockSpec(rates.shape, lambda i: (0, 0))
    feat = pl.BlockSpec((toks, TILE), lambda i: (0, i))
    return pl.pallas_call(
        functools.partial(local_kernel, width),
        grid=(chans // TILE,),
        in_specs=[feat, table, table],
        out_specs=[feat, pl.BlockSpec((2, rows), lambda i: (0, i))],
        out_shape=[
            jax.ShapeDtypeStruct((toks, chans), BF16),
            jax.ShapeDtypeStruct((2, rates.size), F32),
        ],
        scratch_shapes=[
            pltpu.VMEM((SUB, groups * SUB), BF16),
            pltpu.VMEM((groups * SUB, toks // SUB * TILE), BF16),
        ],
        compiler_params=pltpu.CompilerParams(vmem_limit_bytes=VMEM_BYTES),
        cost_estimate=SHORT,
        name="local_conv",
    )(u, rates, residues)


def gate_kernel(modes, width, counts, place_ref, z_ref, q_ref, rows_ref, state_ref, *y_refs):
    y_refs = list(zip(y_refs, counts))
    step = pl.program_id(0)
    entering = jnp.sum(state_ref[...].astype(F32), axis=0)
    first = place_ref[step] * SUB + 1
    rows = TILE // width * modes
    mask = own_mask(rows, TILE, modes, width)
    tiles = []
    for tile in range(q_ref.shape[1] // TILE):
        lanes = slice(tile * TILE, (tile + 1) * TILE)
        group = slice(tile * rows, (tile + 1) * rows)
        after = lax.broadcasted_iota(jnp.int32, (SUB, rows), 0) + first
        readout = (
            rows_ref[1:2, group] * jnp.exp(-rows_ref[0:1, group] * after.astype(F32))
        ).astype(BF16)
        spread = jnp.concatenate([entering[:, lanes]] * (TILE // width), axis=0)
        spread = jnp.where(mask, spread, 0.0).astype(BF16)
        z = z_ref[:, lanes].astype(F32) + dot32(readout, spread)
        tiles.append((q_ref[:, lanes].astype(F32) * z).astype(BF16))
    at = 0
    for y_ref, count in y_refs:

        @pl.when((step >= at) & (step < at + count))
        def _():
            y_ref[...] = jnp.concatenate(tiles, axis=1)

        at += count


def gate(places, counts, z, query_feat, rows, states, width):
    modes, chans = states.shape[1], query_feat.shape[1]
    whole = lambda a: pl.BlockSpec(a.shape, lambda i, p: (0,) * a.ndim)
    block = pl.BlockSpec((SUB, chans), lambda i, p: (p[i], 0))

    def result(first, count):
        return pl.BlockSpec((SUB, chans), lambda i, p: (jnp.clip(i - first, 0, count - 1), 0))

    return pl.pallas_call(
        functools.partial(gate_kernel, modes, width, counts),
        grid_spec=pltpu.PrefetchScalarGridSpec(
            num_scalar_prefetch=1,
            grid=(sum(counts),),
            in_specs=[block, block, whole(rows), whole(states)],
            out_specs=[result(sum(counts[:n]), count) for n, count in enumerate(counts)],
        ),
        out_shape=[jax.ShapeDtypeStruct((n * SUB, chans), BF16) for n in counts],
        compiler_params=pltpu.CompilerParams(vmem_limit_bytes=VMEM_BYTES),
        cost_estimate=SHORT,
        name="gate",
    )(places, z, query_feat, rows, states)


def share_kernel(sets, count, adds, *refs):
    near = jnp.concatenate([r[...] for r in refs[:sets]], axis=0)
    far = jnp.concatenate([r[...] for r in refs[sets : 2 * sets]], axis=0)
    weights = refs[2 * sets :][: 2 * count]
    extra, outs = refs[2 * sets + 2 * count :][: len(adds)], refs[2 * sets + 2 * count + len(adds) :]
    rows, cols = outs[0].shape[0], weights[0].shape[1]
    added = {}
    for ref, at in zip(extra, adds):
        for n in range(ref.shape[1] // cols):
            added[at + n] = ref, n * cols
    for i, (wn, wf) in enumerate(zip(weights[:count], weights[count:])):
        total = dot32(near, wn[...]) + dot32(far, wf[...])
        if i in added:
            ref, n = added[i]
            total = total + ref[:, n : n + cols].astype(F32)
        total = total.astype(BF16)
        for j, out in enumerate(outs):
            out[:, i * cols : (i + 1) * cols] = total[j * rows : (j + 1) * rows]


def share(near, far, near_w, far_w, cols, parts=1, adds=(), cost=SHORT):
    depth = near[0][0].shape[1]
    rows = lambda n: pl.BlockSpec((SUB, depth), lambda i: (n, 0))
    part = lambda col: pl.BlockSpec((depth, cols), lambda i: (0, col))
    whole = lambda *shape: pl.BlockSpec(shape, lambda i: (0, 0))
    height, total = len(near) * SUB, cols * len(near_w)
    return pl.pallas_call(
        functools.partial(share_kernel, len(near), len(near_w), [at for _, at in adds]),
        grid=(1,),
        in_specs=[rows(n) for _, n in near + far]
        + [part(col) for _, col in near_w + far_w]
        + [whole(*a.shape) for a, _ in adds],
        out_specs=[whole(height // parts, total)] * parts,
        out_shape=[jax.ShapeDtypeStruct((height // parts, total), BF16)] * parts,
        compiler_params=pltpu.CompilerParams(vmem_limit_bytes=VMEM_BYTES),
        cost_estimate=cost,
        name="share",
    )(*[a for a, _ in near + far + near_w + far_w], *[a for a, _ in adds])


def place_kernel(spots, place_ref, *refs):
    out_ref, total_ref, sem = refs[-3:]
    cols = total_ref.shape[2]
    copies = []
    for j, spot in enumerate(spots):
        terms = [refs[i][:, n * cols : (n + 1) * cols] for i, n in spot]
        total = terms[0] if len(terms) == 1 else sum(t.astype(F32) for t in terms).astype(BF16)
        total_ref[j] = total
        to = pl.ds(pl.multiple_of(place_ref[j] * cols, cols), cols)
        copies.append(pltpu.make_async_copy(total_ref.at[j], out_ref.at[:, to], sem.at[j]))
        copies[-1].start()
    for copy in copies:
        copy.wait()


def place(places, terms, cols, all_cols):
    arrays, spots = [], []
    for group in terms:
        spot = []
        for array, n in group:
            known = [i for i, a in enumerate(arrays) if a is array]
            if not known:
                known = [len(arrays)]
                arrays.append(array)
            spot.append((known[0], n))
        spots.append(spot)
    rows = arrays[0].shape[0]
    specs = [pl.BlockSpec(a.shape, lambda i, p: (0, 0)) for a in arrays]
    return pl.pallas_call(
        functools.partial(place_kernel, spots),
        grid_spec=pltpu.PrefetchScalarGridSpec(
            num_scalar_prefetch=1,
            grid=(1,),
            in_specs=specs,
            out_specs=pl.BlockSpec(memory_space=pl.ANY),
            scratch_shapes=[
                pltpu.VMEM((len(spots), rows, cols), BF16),
                pltpu.SemaphoreType.DMA((len(spots),)),
            ],
        ),
        out_shape=jax.ShapeDtypeStruct((rows, all_cols), BF16),
        compiler_params=pltpu.CompilerParams(vmem_limit_bytes=63 << 20),
        cost_estimate=SHORT,
        name="place",
    )(places, *arrays)


def arrived_kernel(spots_ref, *refs):
    for i in range(spots_ref.shape[0]):
        refs[-1][i] = spots_ref[i]


def arrived(spots, *arrays):
    smem = pl.BlockSpec(memory_space=pltpu.SMEM)
    return pl.pallas_call(
        arrived_kernel,
        in_specs=[smem] + [pl.BlockSpec(memory_space=pl.ANY)] * len(arrays),
        out_specs=smem,
        out_shape=jax.ShapeDtypeStruct(spots.shape, spots.dtype),
        cost_estimate=LONG,
        name="arrived",
    )(spots, *arrays)


def flip(x, axis, size, bits):
    return lax.ppermute(x, axis, [(i, i ^ bits) for i in range(size)])


def after(x, *others):
    return lax.optimization_barrier((x, *others))[0]


def on_device(seq_size, ch_size, query_feat, key_feat, value_feat, decay_rates, residues, out_weight):
    toks, chans = query_feat.shape
    groups, modes = decay_rates.shape
    width = chans // groups
    piece_cols = out_weight.shape[1]
    all_cols = piece_cols * seq_size
    me = lax.axis_index("seq").astype(jnp.int32)
    plane = lax.axis_index("ch").astype(jnp.int32)
    far_plane = lambda x: flip(x, "ch", ch_size, 2)
    next_plane = lambda x: flip(x, "ch", ch_size, 1)

    rates, residues = decay_rates.T, residues.T
    u, ends = range_state(me.reshape(1), key_feat, value_feat, rates, seq_size, width)
    states = lax.all_to_all(ends, "seq", 0, 0, tiled=True)
    z, rows = local_conv(u, rates, residues, width)

    def gated(slots, counts, *hold):
        places = plane ^ jnp.array(slots, jnp.int32)
        return gate(places, counts, after(z, *hold), query_feat, rows, states, width)

    if seq_size != 8:
        y_3, near, y_2 = gated((3, 1, 0, 2), (1, 2, 1))
        near_w = lax.all_gather(out_weight, "seq", axis=1, tiled=True)
        far_w = lax.all_gather(far_plane(out_weight), "seq", axis=1, tiled=True)
        far_other, far_own = far_plane(y_3), far_plane(y_2)
        near_w, far_w = [(near_w, 0)], [(far_w, 0)]
        (part,) = share([(near, 0)], [(far_other, 0)], near_w, far_w, all_cols)
        (own,) = share([(near, 1)], [(far_own, 0)], near_w, far_w, all_cols)
        return (own.astype(F32) + next_plane(part).astype(F32)).astype(BF16)

    core = lambda x: flip(x, "seq", seq_size, 1)
    pairs = [(s * ch_size + c, (s ^ 1) * ch_size + (c ^ 1)) for s in range(seq_size) for c in range(ch_size)]
    next_cross = lambda x: lax.ppermute(x, ("seq", "ch"), pairs)
    sides = [(2, 4), (4, 2), (6, 6)]

    def over(x, way):
        return lax.ppermute(x, "seq", [(i, i ^ sides[way][i % 2]) for i in range(seq_size)])

    half = piece_cols // 2
    first, second = slice(0, half), slice(half, None)

    n_a = out_weight[:, first]
    f_a = far_plane(n_a)
    n_1 = over(out_weight, 0)
    (y_3,) = gated((3,), (1,), n_1)

    y_far_other = far_plane(y_3)
    f_a = after(f_a, y_3)
    f_a1, f_a2 = over(f_a, 0), over(f_a, 1)
    n_2 = over(after(out_weight, f_a), 1)
    near, y_2 = gated((1, 0, 2), (2, 1), n_1, f_a)
    near_sib = core(near)
    n_b = after(out_weight, near)[:, second]
    y_far_other, f_a1, f_a2, n_2, n_b = lax.optimization_barrier(
        (y_far_other, f_a1, f_a2, n_2, n_b)
    )

    f_b = far_plane(n_b)
    far_other_sib = core(y_far_other)
    n_3, f_a3 = over(after(n_1, far_other_sib), 1), over(after(f_a1, far_other_sib), 1)
    near_w, far_w = [(out_weight, 0), (n_1, 0), (n_2, 0)], [(f_a, 0), (f_a1, 0), (f_a2, 0)]
    near_other, near_own = [(near, 0), (near_sib, 0)], [(near, 1), (near_sib, 1)]
    far_other = [(y_far_other, 0), (far_other_sib, 0)]

    def products(near, far, pieces, **kw):
        return share(near, far, [near_w[i] for i in pieces], [far_w[i] for i in pieces], half, **kw)

    (ready_1,) = products(near_other, far_other, range(3))
    part_1 = next_plane(ready_1)

    f_b, n_3, f_a3 = lax.optimization_barrier((f_b, n_3, f_a3))
    near_w = [(n, h) for h in (0, 1) for n in (out_weight, n_1, n_2, n_3)]
    y_far_own = far_plane(after(y_2, f_b))
    f_b1, f_b2, f_b3 = (over(f_b, way) for way in range(3))
    far_w += [(f_a3, 0), (f_b, 0)]
    (ready_2,) = products(near_other, far_other, range(3, 5))
    part_2 = next_plane(after(ready_2, part_1))
    far_w += [(after(f_b1, y_far_own), 0), (f_b2, 0), (f_b3, 0)]
    mine, other = products(near_other, far_other, range(5, 8), parts=2, cost=LONG)
    part_3 = next_plane(mine), next_cross(other)

    far_own_sib = core(after(y_far_own, mine))
    far_own = [(after(y_far_own, part_2), 0), (far_own_sib, 0)]
    mine, other = products(
        near_own, far_own, range(8), parts=2, adds=[(part_1, 0), (part_2, 3)]
    )
    other = core(other)
    own, cross = [[(mine, n)] for n in range(8)], [[(other, n)] for n in range(8)]
    for n in range(3):
        own[5 + n].append((part_3[0], n))
        cross[5 + n].append((part_3[1], n))

    def spots(s):
        at = me ^ s
        chips = [0, jnp.where(at % 2 == 0, 2, 4), jnp.where(at % 2 == 0, 4, 2), 6]
        return jnp.stack([(at ^ chips[i % 4]) * 2 + i // 4 for i in range(8)])

    at = arrived(jnp.concatenate([spots(0), spots(1)]), *part_3)
    return place(at, own + cross, half, all_cols)


def solution(mesh):
    in_specs = (
        P("seq", "ch"),
        P("seq", "ch"),
        P("seq", "ch"),
        P("ch", None),
        P("ch", None),
        P("ch", "seq"),
    )
    out_specs = P(("seq", "ch"), None)
    body = functools.partial(on_device, mesh.shape["seq"], mesh.shape["ch"])
    return jax.shard_map(
        body, mesh=mesh, in_specs=in_specs, out_specs=out_specs, check_vma=False
    )
```

```python
import functools

import jax
import jax.numpy as jnp
from jax import lax
from jax.experimental import pallas as pl
from jax.experimental.pallas import tpu as pltpu
from jax.sharding import PartitionSpec as P

SUB = 256
TILE = 128
F32 = jnp.float32
BF16 = jnp.bfloat16


def dot32(a, b):
    return jnp.dot(a, b, preferred_element_type=F32)


def own_mask(rows, cols, modes, width):
    r = lax.broadcasted_iota(jnp.int32, (rows, cols), 0) // modes
    c = lax.broadcasted_iota(jnp.int32, (rows, cols), 1) // width
    return r == c


def as_column(table, first, count):
    modes, groups = table.shape
    rows = jnp.broadcast_to(table[None], (count, modes, groups)).reshape(count * modes, groups)
    group = lax.broadcasted_iota(jnp.int32, rows.shape, 0) // modes + first
    pick = group == lax.broadcasted_iota(jnp.int32, rows.shape, 1)
    return jnp.sum(jnp.where(pick, rows, 0.0), axis=1, keepdims=True)


def as_row(column):
    size = column.shape[0]
    same = lax.broadcasted_iota(jnp.int32, (size, size), 0)
    same = same == lax.broadcasted_iota(jnp.int32, (size, size), 1)
    return jnp.sum(jnp.where(same, column, 0.0), axis=0, keepdims=True)


VMEM_BYTES = 56 << 20
SHORT = pl.CostEstimate(flops=1, bytes_accessed=1, transcendentals=0)
LONG = pl.CostEstimate(flops=1 << 36, bytes_accessed=1 << 28, transcendentals=0)


def range_state_kernel(width, me_ref, k_ref, v_ref, rate_ref, u_ref, f_ref):
    u = (k_ref[...].astype(F32) * v_ref[...].astype(F32)).astype(BF16)
    u_ref[...] = u
    toks, cols = u.shape
    modes = rate_ref.shape[0]
    count = cols // width
    rate = as_column(rate_ref[...], pl.program_id(0) * count, count)
    rows = rate.shape[0]
    left = (SUB - 1) - lax.broadcasted_iota(jnp.int32, (rows, SUB), 1)
    inject = jnp.exp(-rate * left.astype(F32)).astype(BF16)
    decay = jnp.exp(-rate * SUB)
    sums = dot32(inject, u[:SUB])
    for n in range(1, toks // SUB):
        sums = decay * sums + dot32(inject, u[n * SUB : (n + 1) * SUB])
    sums = jnp.where(own_mask(rows, cols, modes, width), sums, 0.0)
    for to in range(f_ref.shape[0]):
        lag = to - 1 - me_ref[0]
        weight = jnp.exp(-rate * (jnp.maximum(lag, 0) * toks).astype(F32))
        there = (weight * sums).reshape(rows // modes, modes, cols)
        f_ref[to] = jnp.where(lag >= 0, jnp.sum(there, axis=0), 0.0).astype(BF16)


def range_state(me, key_feat, value_feat, rates, seq_size, width):
    toks, chans = key_feat.shape
    modes = rates.shape[0]
    step = 256
    feat = pl.BlockSpec((toks, step), lambda i, p: (0, i))
    return pl.pallas_call(
        functools.partial(range_state_kernel, width),
        grid_spec=pltpu.PrefetchScalarGridSpec(
            num_scalar_prefetch=1,
            grid=(chans // step,),
            in_specs=[feat, feat, pl.BlockSpec(rates.shape, lambda i, p: (0, 0))],
            out_specs=[feat, pl.BlockSpec((seq_size, modes, step), lambda i, p: (0, 0, i))],
        ),
        out_shape=[
            jax.ShapeDtypeStruct((toks, chans), BF16),
            jax.ShapeDtypeStruct((seq_size, modes, chans), BF16),
        ],
        compiler_params=pltpu.CompilerParams(vmem_limit_bytes=VMEM_BYTES),
        cost_estimate=SHORT,
        name="range_state",
    )(me, key_feat, value_feat, rates)


def local_kernel(width, u_ref, rate_ref, res_ref, z_ref, rows_ref, taps_ref, split_ref):
    modes, groups = rate_ref.shape[0], TILE // width
    rows = groups * modes
    rate, res = (as_column(r[...], pl.program_id(0) * groups, groups) for r in (rate_ref, res_ref))
    rate_row, res_row = as_row(rate), as_row(res)
    rows_ref[0:1, :] = rate_row
    rows_ref[1:2, :] = res_row
    blocks = u_ref.shape[0] // SUB
    lag = 2 * SUB - lax.broadcasted_iota(jnp.int32, (rows, 2 * SUB), 1)
    lag = jnp.where(lag == 2 * SUB, 0, lag)
    terms = jnp.where(lag < SUB, res * jnp.exp(-rate * lag.astype(F32)), 0.0)
    wheel = jnp.sum(terms.reshape(groups, modes, 2 * SUB), axis=1)
    half = SUB // 2
    both = jnp.concatenate([u_ref[n * SUB : (n + 1) * SUB, :] for n in range(blocks)], axis=1)
    lane_group = (lax.broadcasted_iota(jnp.int32, (1, blocks * TILE), 1) % TILE) // width
    for g in range(groups):
        base = jnp.broadcast_to(wheel[g : g + 1], (half, 2 * SUB))
        low = pltpu.roll(base, half, 1, stride=1, stride_axis=0)[:, :SUB].astype(BF16)
        taps_ref[half:, g * SUB : (g + 1) * SUB] = low
        taps_ref[:half, g * SUB : g * SUB + half] = low[:, half:]
        taps_ref[:half, g * SUB + half : (g + 1) * SUB] = jnp.zeros((half, half), BF16)
        split_ref[g * SUB : (g + 1) * SUB, :] = both * (lane_group == g).astype(BF16)

    mask = own_mask(rows, TILE, modes, width)
    left = (SUB - 1) - lax.broadcasted_iota(jnp.int32, (rows, SUB), 1)
    inject = jnp.exp(-rate * left.astype(F32)).astype(BF16)
    sums = dot32(inject, both[:, : (blocks - 1) * TILE])
    decay = jnp.exp(-rate * SUB)
    state, starts = jnp.zeros((rows, TILE), F32), []
    for n in range(blocks - 1):
        own = jnp.where(mask, sums[:, n * TILE : (n + 1) * TILE], 0.0)
        state = decay * state + own
        starts.append(state.astype(BF16))
    after = lax.broadcasted_iota(jnp.int32, (SUB, rows), 0) + 1
    readout = (res_row * jnp.exp(-rate_row * after.astype(F32))).astype(BF16)
    carried = dot32(readout, jnp.concatenate(starts, axis=1))
    z = dot32(taps_ref[...], split_ref[...])
    z_ref[:SUB, :] = z[:, :TILE].astype(BF16)
    for n in range(1, blocks):
        z_ref[n * SUB : (n + 1) * SUB, :] = (
            z[:, n * TILE : (n + 1) * TILE] + carried[:, (n - 1) * TILE : n * TILE]
        ).astype(BF16)


def local_conv(u, rates, residues, width):
    toks, chans = u.shape
    modes = rates.shape[0]
    groups = TILE // width
    rows = groups * modes
    table = pl.BlockSpec(rates.shape, lambda i: (0, 0))
    feat = pl.BlockSpec((toks, TILE), lambda i: (0, i))
    return pl.pallas_call(
        functools.partial(local_kernel, width),
        grid=(chans // TILE,),
        in_specs=[feat, table, table],
        out_specs=[feat, pl.BlockSpec((2, rows), lambda i: (0, i))],
        out_shape=[
            jax.ShapeDtypeStruct((toks, chans), BF16),
            jax.ShapeDtypeStruct((2, rates.size), F32),
        ],
        scratch_shapes=[
            pltpu.VMEM((SUB, groups * SUB), BF16),
            pltpu.VMEM((groups * SUB, toks // SUB * TILE), BF16),
        ],
        compiler_params=pltpu.CompilerParams(vmem_limit_bytes=VMEM_BYTES),
        cost_estimate=SHORT,
        name="local_conv",
    )(u, rates, residues)


def gate_kernel(modes, width, counts, place_ref, z_ref, q_ref, rows_ref, state_ref, *y_refs):
    y_refs = list(zip(y_refs, counts))
    step = pl.program_id(0)
    entering = jnp.sum(state_ref[...].astype(F32), axis=0)
    first = place_ref[step] * SUB + 1
    rows = TILE // width * modes
    mask = own_mask(rows, TILE, modes, width)
    tiles = []
    for tile in range(q_ref.shape[1] // TILE):
        lanes = slice(tile * TILE, (tile + 1) * TILE)
        group = slice(tile * rows, (tile + 1) * rows)
        after = lax.broadcasted_iota(jnp.int32, (SUB, rows), 0) + first
        readout = (
            rows_ref[1:2, group] * jnp.exp(-rows_ref[0:1, group] * after.astype(F32))
        ).astype(BF16)
        spread = jnp.concatenate([entering[:, lanes]] * (TILE // width), axis=0)
        spread = jnp.where(mask, spread, 0.0).astype(BF16)
        z = z_ref[:, lanes].astype(F32) + dot32(readout, spread)
        tiles.append((q_ref[:, lanes].astype(F32) * z).astype(BF16))
    at = 0
    for y_ref, count in y_refs:

        @pl.when((step >= at) & (step < at + count))
        def _():
            y_ref[...] = jnp.concatenate(tiles, axis=1)

        at += count


def gate(places, counts, z, query_feat, rows, states, width):
    modes, chans = states.shape[1], query_feat.shape[1]
    whole = lambda a: pl.BlockSpec(a.shape, lambda i, p: (0,) * a.ndim)
    block = pl.BlockSpec((SUB, chans), lambda i, p: (p[i], 0))

    def result(first, count):
        return pl.BlockSpec((SUB, chans), lambda i, p: (jnp.clip(i - first, 0, count - 1), 0))

    return pl.pallas_call(
        functools.partial(gate_kernel, modes, width, counts),
        grid_spec=pltpu.PrefetchScalarGridSpec(
            num_scalar_prefetch=1,
            grid=(sum(counts),),
            in_specs=[block, block, whole(rows), whole(states)],
            out_specs=[result(sum(counts[:n]), count) for n, count in enumerate(counts)],
        ),
        out_shape=[jax.ShapeDtypeStruct((n * SUB, chans), BF16) for n in counts],
        compiler_params=pltpu.CompilerParams(vmem_limit_bytes=VMEM_BYTES),
        cost_estimate=SHORT,
        name="gate",
    )(places, z, query_feat, rows, states)


def share_kernel(sets, count, adds, *refs):
    near = jnp.concatenate([r[...] for r in refs[:sets]], axis=0)
    far = jnp.concatenate([r[...] for r in refs[sets : 2 * sets]], axis=0)
    weights = refs[2 * sets :][: 2 * count]
    extra, outs = refs[2 * sets + 2 * count :][: len(adds)], refs[2 * sets + 2 * count + len(adds) :]
    rows, cols = outs[0].shape[0], weights[0].shape[1]
    added = {}
    for ref, at in zip(extra, adds):
        for n in range(ref.shape[1] // cols):
            added[at + n] = ref, n * cols
    for i, (wn, wf) in enumerate(zip(weights[:count], weights[count:])):
        total = dot32(near, wn[...]) + dot32(far, wf[...])
        if i in added:
            ref, n = added[i]
            total = total + ref[:, n : n + cols].astype(F32)
        total = total.astype(BF16)
        for j, out in enumerate(outs):
            out[:, i * cols : (i + 1) * cols] = total[j * rows : (j + 1) * rows]


def share(near, far, near_w, far_w, cols, parts=1, adds=(), cost=SHORT):
    depth = near[0][0].shape[1]
    rows = lambda n: pl.BlockSpec((SUB, depth), lambda i: (n, 0))
    part = lambda col: pl.BlockSpec((depth, cols), lambda i: (0, col))
    whole = lambda *shape: pl.BlockSpec(shape, lambda i: (0, 0))
    height, total = len(near) * SUB, cols * len(near_w)
    return pl.pallas_call(
        functools.partial(share_kernel, len(near), len(near_w), [at for _, at in adds]),
        grid=(1,),
        in_specs=[rows(n) for _, n in near + far]
        + [part(col) for _, col in near_w + far_w]
        + [whole(*a.shape) for a, _ in adds],
        out_specs=[whole(height // parts, total)] * parts,
        out_shape=[jax.ShapeDtypeStruct((height // parts, total), BF16)] * parts,
        compiler_params=pltpu.CompilerParams(vmem_limit_bytes=63 << 20),
        cost_estimate=cost,
        name="share",
    )(*[a for a, _ in near + far + near_w + far_w], *[a for a, _ in adds])


def place_kernel(spots, place_ref, *refs):
    out_ref, total_ref, sem = refs[-3:]
    cols = total_ref.shape[2]
    copies = []
    for j, spot in enumerate(spots):
        terms = [refs[i][:, n * cols : (n + 1) * cols] for i, n in spot]
        total = terms[0] if len(terms) == 1 else sum(t.astype(F32) for t in terms).astype(BF16)
        total_ref[j] = total
        to = pl.ds(pl.multiple_of(place_ref[j] * cols, cols), cols)
        copies.append(pltpu.make_async_copy(total_ref.at[j], out_ref.at[:, to], sem.at[j]))
        copies[-1].start()
    for copy in copies:
        copy.wait()


def place(places, terms, cols, all_cols, out=None):
    arrays, spots = [], []
    for group in terms:
        spot = []
        for array, n in group:
            known = [i for i, a in enumerate(arrays) if a is array]
            if not known:
                known = [len(arrays)]
                arrays.append(array)
            spot.append((known[0], n))
        spots.append(spot)
    rows = arrays[0].shape[0]
    specs = [pl.BlockSpec(a.shape, lambda i, p: (0, 0)) for a in arrays]
    alias = {}
    if out is not None:
        alias = {1 + len(arrays): 0}
        arrays.append(out)
        specs.append(pl.BlockSpec(memory_space=pl.ANY))
    return pl.pallas_call(
        functools.partial(place_kernel, spots),
        grid_spec=pltpu.PrefetchScalarGridSpec(
            num_scalar_prefetch=1,
            grid=(1,),
            in_specs=specs,
            out_specs=pl.BlockSpec(memory_space=pl.ANY),
            scratch_shapes=[
                pltpu.VMEM((len(spots), rows, cols), BF16),
                pltpu.SemaphoreType.DMA((len(spots),)),
            ],
        ),
        out_shape=jax.ShapeDtypeStruct((rows, all_cols), BF16),
        input_output_aliases=alias,
        compiler_params=pltpu.CompilerParams(vmem_limit_bytes=63 << 20),
        cost_estimate=SHORT,
        name="place",
    )(places, *arrays)


def arrived_kernel(spots_ref, *refs):
    for i in range(spots_ref.shape[0]):
        refs[-1][i] = spots_ref[i]


def arrived(spots, *arrays):
    smem = pl.BlockSpec(memory_space=pltpu.SMEM)
    return pl.pallas_call(
        arrived_kernel,
        in_specs=[smem] + [pl.BlockSpec(memory_space=pl.ANY)] * len(arrays),
        out_specs=smem,
        out_shape=jax.ShapeDtypeStruct(spots.shape, spots.dtype),
        cost_estimate=LONG,
        name="arrived",
    )(spots, *arrays)


def flip(x, axis, size, bits):
    return lax.ppermute(x, axis, [(i, i ^ bits) for i in range(size)])


def after(x, *others):
    return lax.optimization_barrier((x, *others))[0]


def on_device(seq_size, ch_size, query_feat, key_feat, value_feat, decay_rates, residues, out_weight):
    toks, chans = query_feat.shape
    groups, modes = decay_rates.shape
    width = chans // groups
    piece_cols = out_weight.shape[1]
    all_cols = piece_cols * seq_size
    me = lax.axis_index("seq").astype(jnp.int32)
    plane = lax.axis_index("ch").astype(jnp.int32)
    far_plane = lambda x: flip(x, "ch", ch_size, 2)
    next_plane = lambda x: flip(x, "ch", ch_size, 1)

    rates, residues = decay_rates.T, residues.T
    u, ends = range_state(me.reshape(1), key_feat, value_feat, rates, seq_size, width)
    states = lax.all_to_all(ends, "seq", 0, 0, tiled=True)
    z, rows = local_conv(u, rates, residues, width)

    def gated(slots, counts, *hold):
        places = plane ^ jnp.array(slots, jnp.int32)
        return gate(places, counts, after(z, *hold), query_feat, rows, states, width)

    if seq_size != 8:
        y_3, near, y_2 = gated((3, 1, 0, 2), (1, 2, 1))
        near_w = lax.all_gather(out_weight, "seq", axis=1, tiled=True)
        far_w = lax.all_gather(far_plane(out_weight), "seq", axis=1, tiled=True)
        far_other, far_own = far_plane(y_3), far_plane(y_2)
        near_w, far_w = [(near_w, 0)], [(far_w, 0)]
        (part,) = share([(near, 0)], [(far_other, 0)], near_w, far_w, all_cols)
        (own,) = share([(near, 1)], [(far_own, 0)], near_w, far_w, all_cols)
        return (own.astype(F32) + next_plane(part).astype(F32)).astype(BF16)

    core = lambda x: flip(x, "seq", seq_size, 1)
    pairs = [(s * ch_size + c, (s ^ 1) * ch_size + (c ^ 1)) for s in range(seq_size) for c in range(ch_size)]
    next_cross = lambda x: lax.ppermute(x, ("seq", "ch"), pairs)
    sides = [(2, 4), (4, 2), (6, 6)]

    def over(x, way):
        return lax.ppermute(x, "seq", [(i, i ^ sides[way][i % 2]) for i in range(seq_size)])

    half = piece_cols // 2
    first, second = slice(0, half), slice(half, None)

    n_a = out_weight[:, first]
    f_a = far_plane(n_a)
    n_1 = over(out_weight, 0)
    (y_3,) = gated((3,), (1,), n_1)

    y_far_other = far_plane(y_3)
    f_a = after(f_a, y_3)
    f_a1, f_a2 = over(f_a, 0), over(f_a, 1)
    n_2 = over(after(out_weight, f_a), 1)
    n_b = after(out_weight, y_3)[:, second]
    near, y_2 = gated((1, 0, 2), (2, 1), n_1, f_a, n_b)
    near_sib = core(near)
    y_far_other, f_a1, f_a2, n_2, n_b = lax.optimization_barrier(
        (y_far_other, f_a1, f_a2, n_2, n_b)
    )

    f_b = far_plane(n_b)
    far_other_sib = core(y_far_other)
    n_3, f_a3 = over(after(n_1, y_far_other), 1), over(after(f_a1, y_far_other), 1)
    near_w, far_w = [(out_weight, 0), (n_1, 0), (n_2, 0)], [(f_a, 0), (f_a1, 0), (f_a2, 0)]
    near_other, near_own = [(near, 0), (near_sib, 0)], [(near, 1), (near_sib, 1)]
    far_other = [(y_far_other, 0), (far_other_sib, 0)]

    def products(near, far, pieces, **kw):
        return share(near, far, [near_w[i] for i in pieces], [far_w[i] for i in pieces], half, **kw)

    (ready_1,) = products(near_other, far_other, range(3))
    part_1 = next_plane(ready_1)

    f_b, n_3, f_a3 = lax.optimization_barrier((f_b, n_3, f_a3))
    near_w = [(n, h) for h in (0, 1) for n in (out_weight, n_1, n_2, n_3)]
    y_far_own = far_plane(after(y_2, f_b))
    f_b1, f_b2, f_b3 = (over(f_b, way) for way in range(3))
    far_w += [(f_a3, 0), (f_b, 0)]
    (ready_2,) = products(near_other, far_other, range(3, 5))
    part_2 = next_plane(after(ready_2, part_1))
    far_w += [(after(f_b1, y_far_own), 0), (f_b2, 0), (f_b3, 0)]
    mine, other = products(near_other, far_other, range(5, 8), parts=2, cost=LONG)
    part_3 = next_plane(mine), next_cross(other)

    far_own_sib = core(after(y_far_own, mine))
    far_own = [(after(y_far_own, part_2), 0), (far_own_sib, 0)]
    mine, other = products(
        near_own, far_own, range(8), parts=2, adds=[(part_1, 0), (part_2, 3)]
    )
    other = core(other)
    own, cross = [[(mine, n)] for n in range(8)], [[(other, n)] for n in range(8)]
    for n in range(3):
        own[5 + n].append((part_3[0], n))
        cross[5 + n].append((part_3[1], n))

    def spots(s):
        at = me ^ s
        chips = [0, jnp.where(at % 2 == 0, 2, 4), jnp.where(at % 2 == 0, 4, 2), 6]
        return jnp.stack([(at ^ chips[i % 4]) * 2 + i // 4 for i in range(8)])

    early = place(spots(0)[:5], own[:5], half, all_cols)
    at = arrived(jnp.concatenate([spots(0)[5:], spots(1)]), *part_3, early)
    return place(at, own[5:] + cross, half, all_cols, early)


def solution(mesh):
    in_specs = (
        P("seq", "ch"),
        P("seq", "ch"),
        P("seq", "ch"),
        P("ch", None),
        P("ch", None),
        P("ch", "seq"),
    )
    out_specs = P(("seq", "ch"), None)
    body = functools.partial(on_device, mesh.shape["seq"], mesh.shape["ch"])
    return jax.shard_map(
        body, mesh=mesh, in_specs=in_specs, out_specs=out_specs, check_vma=False
    )
```

```python
import functools

import jax
import jax.numpy as jnp
from jax import lax
from jax.experimental import pallas as pl
from jax.experimental.pallas import tpu as pltpu
from jax.sharding import PartitionSpec as P

SUB = 256
TILE = 128
F32 = jnp.float32
BF16 = jnp.bfloat16


def dot32(a, b):
    return jnp.dot(a, b, preferred_element_type=F32)


def own_mask(rows, cols, modes, width):
    r = lax.broadcasted_iota(jnp.int32, (rows, cols), 0) // modes
    c = lax.broadcasted_iota(jnp.int32, (rows, cols), 1) // width
    return r == c


def as_column(table, first, count):
    modes, groups = table.shape
    rows = jnp.broadcast_to(table[None], (count, modes, groups)).reshape(count * modes, groups)
    group = lax.broadcasted_iota(jnp.int32, rows.shape, 0) // modes + first
    pick = group == lax.broadcasted_iota(jnp.int32, rows.shape, 1)
    return jnp.sum(jnp.where(pick, rows, 0.0), axis=1, keepdims=True)


def as_row(column):
    size = column.shape[0]
    same = lax.broadcasted_iota(jnp.int32, (size, size), 0)
    same = same == lax.broadcasted_iota(jnp.int32, (size, size), 1)
    return jnp.sum(jnp.where(same, column, 0.0), axis=0, keepdims=True)


VMEM_BYTES = 56 << 20
SHORT = pl.CostEstimate(flops=1, bytes_accessed=1, transcendentals=0)
LONG = pl.CostEstimate(flops=1 << 36, bytes_accessed=1 << 28, transcendentals=0)


def range_state_kernel(width, me_ref, k_ref, v_ref, rate_ref, u_ref, f_ref):
    u = k_ref[...] * v_ref[...]
    u_ref[...] = u
    toks, cols = u.shape
    modes = rate_ref.shape[0]
    count = cols // width
    rate = as_column(rate_ref[...], pl.program_id(0) * count, count)
    rows = rate.shape[0]
    left = (SUB - 1) - lax.broadcasted_iota(jnp.int32, (rows, SUB), 1)
    inject = jnp.exp(-rate * left.astype(F32)).astype(BF16)
    decay = jnp.exp(-rate * SUB)
    sums = dot32(inject, u[:SUB])
    for n in range(1, toks // SUB):
        sums = decay * sums + dot32(inject, u[n * SUB : (n + 1) * SUB])
    sums = jnp.where(own_mask(rows, cols, modes, width), sums, 0.0)
    for to in range(f_ref.shape[0]):
        lag = to - 1 - me_ref[0]
        weight = jnp.exp(-rate * (jnp.maximum(lag, 0) * toks).astype(F32))
        there = (weight * sums).reshape(rows // modes, modes, cols)
        f_ref[to] = jnp.where(lag >= 0, jnp.sum(there, axis=0), 0.0).astype(BF16)


def range_state(me, key_feat, value_feat, rates, seq_size, width):
    toks, chans = key_feat.shape
    modes = rates.shape[0]
    step = 256
    feat = pl.BlockSpec((toks, step), lambda i, p: (0, i))
    return pl.pallas_call(
        functools.partial(range_state_kernel, width),
        grid_spec=pltpu.PrefetchScalarGridSpec(
            num_scalar_prefetch=1,
            grid=(chans // step,),
            in_specs=[feat, feat, pl.BlockSpec(rates.shape, lambda i, p: (0, 0))],
            out_specs=[feat, pl.BlockSpec((seq_size, modes, step), lambda i, p: (0, 0, i))],
        ),
        out_shape=[
            jax.ShapeDtypeStruct((toks, chans), BF16),
            jax.ShapeDtypeStruct((seq_size, modes, chans), BF16),
        ],
        compiler_params=pltpu.CompilerParams(vmem_limit_bytes=VMEM_BYTES),
        cost_estimate=SHORT,
        name="range_state",
    )(me, key_feat, value_feat, rates)


def local_tile(width, tile, u_ref, rate_ref, res_ref, z_ref, rows_ref, taps_ref, split_ref):
    modes, groups = rate_ref.shape[0], TILE // width
    rows = groups * modes
    rate, res = (as_column(r[...], tile * groups, groups) for r in (rate_ref, res_ref))
    rate_row, res_row = as_row(rate), as_row(res)
    rows_ref[0:1, :] = rate_row
    rows_ref[1:2, :] = res_row
    blocks = u_ref.shape[0] // SUB
    lag = 2 * SUB - lax.broadcasted_iota(jnp.int32, (rows, 2 * SUB), 1)
    lag = jnp.where(lag == 2 * SUB, 0, lag)
    terms = jnp.where(lag < SUB, res * jnp.exp(-rate * lag.astype(F32)), 0.0)
    wheel = jnp.sum(terms.reshape(groups, modes, 2 * SUB), axis=1)
    half = SUB // 2
    both = jnp.concatenate([u_ref[n * SUB : (n + 1) * SUB, :] for n in range(blocks)], axis=1)
    lane_group = (lax.broadcasted_iota(jnp.int32, (1, blocks * TILE), 1) % TILE) // width
    for g in range(groups):
        base = jnp.broadcast_to(wheel[g : g + 1], (half, 2 * SUB))
        low = pltpu.roll(base, half, 1, stride=1, stride_axis=0)[:, :SUB].astype(BF16)
        taps_ref[half:, g * SUB : (g + 1) * SUB] = low
        taps_ref[:half, g * SUB : g * SUB + half] = low[:, half:]
        taps_ref[:half, g * SUB + half : (g + 1) * SUB] = jnp.zeros((half, half), BF16)
        split_ref[g * SUB : (g + 1) * SUB, :] = both * (lane_group == g).astype(BF16)

    mask = own_mask(rows, TILE, modes, width)
    left = (SUB - 1) - lax.broadcasted_iota(jnp.int32, (rows, SUB), 1)
    inject = jnp.exp(-rate * left.astype(F32)).astype(BF16)
    sums = dot32(inject, both[:, : (blocks - 1) * TILE])
    decay = jnp.exp(-rate * SUB)
    state, starts = jnp.zeros((rows, TILE), F32), []
    for n in range(blocks - 1):
        own = jnp.where(mask, sums[:, n * TILE : (n + 1) * TILE], 0.0)
        state = decay * state + own
        starts.append(state.astype(BF16))
    after = lax.broadcasted_iota(jnp.int32, (SUB, rows), 0) + 1
    readout = (res_row * jnp.exp(-rate_row * after.astype(F32))).astype(BF16)
    carried = dot32(readout, jnp.concatenate(starts, axis=1))
    z = dot32(taps_ref[...], split_ref[...])
    z_ref[:SUB, :] = z[:, :TILE].astype(BF16)
    for n in range(1, blocks):
        z_ref[n * SUB : (n + 1) * SUB, :] = (
            z[:, n * TILE : (n + 1) * TILE] + carried[:, (n - 1) * TILE : n * TILE]
        ).astype(BF16)


def local_kernel(width, u_ref, rate_ref, res_ref, z_ref, rows_ref, taps_ref, split_ref):
    tiles = u_ref.shape[1] // TILE
    per_tile = rows_ref.shape[1] // tiles
    for t in range(tiles):
        lanes = pl.ds(t * TILE, TILE)
        local_tile(
            width, pl.program_id(0) * tiles + t, u_ref.at[:, lanes], rate_ref, res_ref, z_ref.at[:, lanes],
            rows_ref.at[:, pl.ds(t * per_tile, per_tile)], taps_ref.at[t], split_ref.at[t],
        )


def local_conv(u, rates, residues, width):
    toks, chans = u.shape
    modes = rates.shape[0]
    groups = TILE // width
    rows, tiles = groups * modes, 2
    table = pl.BlockSpec(rates.shape, lambda i: (0, 0))
    feat = pl.BlockSpec((toks, tiles * TILE), lambda i: (0, i))
    return pl.pallas_call(
        functools.partial(local_kernel, width),
        grid=(chans // TILE // tiles,),
        in_specs=[feat, table, table],
        out_specs=[feat, pl.BlockSpec((2, tiles * rows), lambda i: (0, i))],
        out_shape=[
            jax.ShapeDtypeStruct((toks, chans), BF16),
            jax.ShapeDtypeStruct((2, rates.size), F32),
        ],
        scratch_shapes=[
            pltpu.VMEM((tiles, SUB, groups * SUB), BF16),
            pltpu.VMEM((tiles, groups * SUB, toks // SUB * TILE), BF16),
        ],
        compiler_params=pltpu.CompilerParams(vmem_limit_bytes=VMEM_BYTES),
        cost_estimate=SHORT,
        name="local_conv",
    )(u, rates, residues)


def gate_kernel(modes, width, counts, place_ref, z_ref, q_ref, rows_ref, state_ref, *y_refs):
    y_refs = list(zip(y_refs, counts))
    step = pl.program_id(0)
    entering = jnp.sum(state_ref[...].astype(F32), axis=0)
    first = place_ref[step] * SUB + 1
    rows = TILE // width * modes
    mask = own_mask(rows, TILE, modes, width)
    tiles = []
    for tile in range(q_ref.shape[1] // TILE):
        lanes = slice(tile * TILE, (tile + 1) * TILE)
        group = slice(tile * rows, (tile + 1) * rows)
        after = lax.broadcasted_iota(jnp.int32, (SUB, rows), 0) + first
        readout = (
            rows_ref[1:2, group] * jnp.exp(-rows_ref[0:1, group] * after.astype(F32))
        ).astype(BF16)
        spread = jnp.concatenate([entering[:, lanes]] * (TILE // width), axis=0)
        spread = jnp.where(mask, spread, 0.0).astype(BF16)
        z = z_ref[:, lanes].astype(F32) + dot32(readout, spread)
        tiles.append((q_ref[:, lanes].astype(F32) * z).astype(BF16))
    at = 0
    for y_ref, count in y_refs:

        @pl.when((step >= at) & (step < at + count))
        def _():
            y_ref[...] = jnp.concatenate(tiles, axis=1)

        at += count


def gate(places, counts, z, query_feat, rows, states, width):
    modes, chans = states.shape[1], query_feat.shape[1]
    whole = lambda a: pl.BlockSpec(a.shape, lambda i, p: (0,) * a.ndim)
    block = pl.BlockSpec((SUB, chans), lambda i, p: (p[i], 0))

    def result(first, count):
        return pl.BlockSpec((SUB, chans), lambda i, p: (jnp.clip(i - first, 0, count - 1), 0))

    return pl.pallas_call(
        functools.partial(gate_kernel, modes, width, counts),
        grid_spec=pltpu.PrefetchScalarGridSpec(
            num_scalar_prefetch=1,
            grid=(sum(counts),),
            in_specs=[block, block, whole(rows), whole(states)],
            out_specs=[result(sum(counts[:n]), count) for n, count in enumerate(counts)],
        ),
        out_shape=[jax.ShapeDtypeStruct((n * SUB, chans), BF16) for n in counts],
        compiler_params=pltpu.CompilerParams(vmem_limit_bytes=VMEM_BYTES),
        cost_estimate=SHORT,
        name="gate",
    )(places, z, query_feat, rows, states)


def share_kernel(sets, count, adds, *refs):
    near = jnp.concatenate([r[...] for r in refs[:sets]], axis=0)
    far = jnp.concatenate([r[...] for r in refs[sets : 2 * sets]], axis=0)
    weights = refs[2 * sets :][: 2 * count]
    extra, outs = refs[2 * sets + 2 * count :][: len(adds)], refs[2 * sets + 2 * count + len(adds) :]
    rows, cols = outs[0].shape[0], weights[0].shape[1]
    added = {}
    for ref, at in zip(extra, adds):
        for n in range(ref.shape[1] // cols):
            added[at + n] = ref, n * cols
    for i, (wn, wf) in enumerate(zip(weights[:count], weights[count:])):
        total = dot32(near, wn[...]) + dot32(far, wf[...])
        if i in added:
            ref, n = added[i]
            total = total + ref[:, n : n + cols].astype(F32)
        total = total.astype(BF16)
        for j, out in enumerate(outs):
            out[:, i * cols : (i + 1) * cols] = total[j * rows : (j + 1) * rows]


def share(near, far, near_w, far_w, cols, parts=1, adds=(), cost=SHORT):
    depth = near[0][0].shape[1]
    rows = lambda n: pl.BlockSpec((SUB, depth), lambda i: (n, 0))
    part = lambda col: pl.BlockSpec((depth, cols), lambda i: (0, col))
    whole = lambda *shape: pl.BlockSpec(shape, lambda i: (0, 0))
    height, total = len(near) * SUB, cols * len(near_w)
    return pl.pallas_call(
        functools.partial(share_kernel, len(near), len(near_w), [at for _, at in adds]),
        grid=(1,),
        in_specs=[rows(n) for _, n in near + far]
        + [part(col) for _, col in near_w + far_w]
        + [whole(*a.shape) for a, _ in adds],
        out_specs=[whole(height // parts, total)] * parts,
        out_shape=[jax.ShapeDtypeStruct((height // parts, total), BF16)] * parts,
        compiler_params=pltpu.CompilerParams(vmem_limit_bytes=63 << 20),
        cost_estimate=cost,
        name="share",
    )(*[a for a, _ in near + far + near_w + far_w], *[a for a, _ in adds])


def place_kernel(spots, place_ref, *refs):
    out_ref, total_ref, sem = refs[-3:]
    cols = total_ref.shape[2]
    copies = []
    for j, spot in enumerate(spots):
        terms = [refs[i][:, n * cols : (n + 1) * cols] for i, n in spot]
        total = terms[0] if len(terms) == 1 else sum(t.astype(F32) for t in terms).astype(BF16)
        total_ref[j] = total
        to = pl.ds(pl.multiple_of(place_ref[j] * cols, cols), cols)
        copies.append(pltpu.make_async_copy(total_ref.at[j], out_ref.at[:, to], sem.at[j]))
        copies[-1].start()
    for copy in copies:
        copy.wait()


def place(places, terms, cols, all_cols, out=None):
    arrays, spots = [], []
    for group in terms:
        spot = []
        for array, n in group:
            known = [i for i, a in enumerate(arrays) if a is array]
            if not known:
                known = [len(arrays)]
                arrays.append(array)
            spot.append((known[0], n))
        spots.append(spot)
    rows = arrays[0].shape[0]
    specs = [pl.BlockSpec(a.shape, lambda i, p: (0, 0)) for a in arrays]
    alias = {}
    if out is not None:
        alias = {1 + len(arrays): 0}
        arrays.append(out)
        specs.append(pl.BlockSpec(memory_space=pl.ANY))
    return pl.pallas_call(
        functools.partial(place_kernel, spots),
        grid_spec=pltpu.PrefetchScalarGridSpec(
            num_scalar_prefetch=1,
            grid=(1,),
            in_specs=specs,
            out_specs=pl.BlockSpec(memory_space=pl.ANY),
            scratch_shapes=[
                pltpu.VMEM((len(spots), rows, cols), BF16),
                pltpu.SemaphoreType.DMA((len(spots),)),
            ],
        ),
        out_shape=jax.ShapeDtypeStruct((rows, all_cols), BF16),
        input_output_aliases=alias,
        compiler_params=pltpu.CompilerParams(vmem_limit_bytes=63 << 20),
        cost_estimate=SHORT,
        name="place",
    )(places, *arrays)


def arrived_kernel(spots_ref, *refs):
    for i in range(spots_ref.shape[0]):
        refs[-1][i] = spots_ref[i]


def arrived(spots, *arrays):
    smem = pl.BlockSpec(memory_space=pltpu.SMEM)
    return pl.pallas_call(
        arrived_kernel,
        in_specs=[smem] + [pl.BlockSpec(memory_space=pl.ANY)] * len(arrays),
        out_specs=smem,
        out_shape=jax.ShapeDtypeStruct(spots.shape, spots.dtype),
        cost_estimate=LONG,
        name="arrived",
    )(spots, *arrays)


def flip(x, axis, size, bits):
    return lax.ppermute(x, axis, [(i, i ^ bits) for i in range(size)])


def after(x, *others):
    return lax.optimization_barrier((x, *others))[0]


def on_device(seq_size, ch_size, query_feat, key_feat, value_feat, decay_rates, residues, out_weight):
    toks, chans = query_feat.shape
    groups, modes = decay_rates.shape
    width = chans // groups
    piece_cols = out_weight.shape[1]
    all_cols = piece_cols * seq_size
    me = lax.axis_index("seq").astype(jnp.int32)
    plane = lax.axis_index("ch").astype(jnp.int32)
    far_plane = lambda x: flip(x, "ch", ch_size, 2)
    next_plane = lambda x: flip(x, "ch", ch_size, 1)

    rates, residues = decay_rates.T, residues.T
    u, ends = range_state(me.reshape(1), key_feat, value_feat, rates, seq_size, width)
    states = lax.all_to_all(ends, "seq", 0, 0, tiled=True)
    z, rows = local_conv(u, rates, residues, width)

    def gated(slots, counts, *hold):
        places = plane ^ jnp.array(slots, jnp.int32)
        return gate(places, counts, after(z, *hold), query_feat, rows, states, width)

    if seq_size != 8:
        y_3, near, y_2 = gated((3, 1, 0, 2), (1, 2, 1))
        near_w = lax.all_gather(out_weight, "seq", axis=1, tiled=True)
        far_w = lax.all_gather(far_plane(out_weight), "seq", axis=1, tiled=True)
        far_other, far_own = far_plane(y_3), far_plane(y_2)
        near_w, far_w = [(near_w, 0)], [(far_w, 0)]
        (part,) = share([(near, 0)], [(far_other, 0)], near_w, far_w, all_cols)
        (own,) = share([(near, 1)], [(far_own, 0)], near_w, far_w, all_cols)
        return (own.astype(F32) + next_plane(part).astype(F32)).astype(BF16)

    core = lambda x: flip(x, "seq", seq_size, 1)
    pairs = [(s * ch_size + c, (s ^ 1) * ch_size + (c ^ 1)) for s in range(seq_size) for c in range(ch_size)]
    next_cross = lambda x: lax.ppermute(x, ("seq", "ch"), pairs)
    sides = [(2, 4), (4, 2), (6, 6)]

    def over(x, way):
        return lax.ppermute(x, "seq", [(i, i ^ sides[way][i % 2]) for i in range(seq_size)])

    half = piece_cols // 2
    first, second = slice(0, half), slice(half, None)

    n_a = out_weight[:, first]
    f_a = far_plane(n_a)
    n_1 = over(out_weight, 0)
    (y_3,) = gated((3,), (1,), n_1)

    y_far_other = far_plane(after(y_3, f_a))
    f_a = after(f_a, y_3)
    f_a1, f_a2 = over(f_a, 0), over(f_a, 1)
    n_2 = over(after(out_weight, f_a), 1)
    n_b = after(out_weight, y_3)[:, second]
    near, y_2 = gated((1, 0, 2), (2, 1), n_1, f_a, n_b)
    near_sib = core(near)
    there = arrived(me.reshape(1), y_far_other)
    f_a1, f_a2, n_2, _ = lax.optimization_barrier((f_a1, f_a2, n_2, there))
    n_b = after(n_b, y_far_other)

    f_b = far_plane(n_b)
    far_other_sib = core(y_far_other)
    n_3, f_a3 = over(after(n_1, there), 1), over(after(f_a1, there), 1)
    near_w, far_w = [(out_weight, 0), (n_1, 0), (n_2, 0)], [(f_a, 0), (f_a1, 0), (f_a2, 0)]
    near_other, near_own = [(near, 0), (near_sib, 0)], [(near, 1), (near_sib, 1)]
    far_other = [(y_far_other, 0), (far_other_sib, 0)]

    def products(near, far, pieces, **kw):
        return share(near, far, [near_w[i] for i in pieces], [far_w[i] for i in pieces], half, **kw)

    (ready_1,) = products(near_other, far_other, range(3))
    part_1 = next_plane(ready_1)

    f_b, n_3, f_a3 = lax.optimization_barrier((f_b, n_3, f_a3))
    near_w = [(n, h) for h in (0, 1) for n in (out_weight, n_1, n_2, n_3)]
    y_far_own = far_plane(after(y_2, f_b))
    f_b1, f_b2, f_b3 = (over(f_b, way) for way in range(3))
    far_w += [(f_a3, 0), (f_b, 0)]
    (ready_2,) = products(near_other, far_other, range(3, 5))
    part_2 = next_plane(after(ready_2, part_1))
    far_w += [(after(f_b1, y_far_own), 0), (f_b2, 0), (f_b3, 0)]
    mine, other = products(near_other, far_other, range(5, 8), parts=2, cost=LONG)
    part_3 = next_plane(mine), next_cross(other)

    far_own_sib = core(after(y_far_own, mine))
    far_own = [(after(y_far_own, part_2), 0), (far_own_sib, 0)]
    mine, other = products(
        near_own, far_own, range(8), parts=2, adds=[(part_1, 0), (part_2, 3)]
    )
    other = core(other)
    own, cross = [[(mine, n)] for n in range(8)], [[(other, n)] for n in range(8)]
    for n in range(3):
        own[5 + n].append((part_3[0], n))
        cross[5 + n].append((part_3[1], n))

    def spots(s):
        at = me ^ s
        chips = [0, jnp.where(at % 2 == 0, 2, 4), jnp.where(at % 2 == 0, 4, 2), 6]
        return jnp.stack([(at ^ chips[i % 4]) * 2 + i // 4 for i in range(8)])

    early = place(spots(0)[:5], own[:5], half, all_cols)
    at = arrived(jnp.concatenate([spots(0)[5:], spots(1)]), *part_3, early)
    return place(at, own[5:] + cross, half, all_cols, early)


def solution(mesh):
    in_specs = (
        P("seq", "ch"),
        P("seq", "ch"),
        P("seq", "ch"),
        P("ch", None),
        P("ch", None),
        P("ch", "seq"),
    )
    out_specs = P(("seq", "ch"), None)
    body = functools.partial(on_device, mesh.shape["seq"], mesh.shape["ch"])
    return jax.shard_map(
        body, mesh=mesh, in_specs=in_specs, out_specs=out_specs, check_vma=False
    )
```

```python
import functools

import jax
import jax.numpy as jnp
from jax import lax
from jax.experimental import pallas as pl
from jax.experimental.pallas import tpu as pltpu
from jax.sharding import PartitionSpec as P

SUB = 256
TILE = 128
F32 = jnp.float32
BF16 = jnp.bfloat16


def dot32(a, b):
    return jnp.dot(a, b, preferred_element_type=F32)


def own_mask(rows, cols, modes, width):
    r = lax.broadcasted_iota(jnp.int32, (rows, cols), 0) // modes
    c = lax.broadcasted_iota(jnp.int32, (rows, cols), 1) // width
    return r == c


def as_column(table, first, count):
    modes, groups = table.shape
    rows = jnp.broadcast_to(table[None], (count, modes, groups)).reshape(count * modes, groups)
    group = lax.broadcasted_iota(jnp.int32, rows.shape, 0) // modes + first
    pick = group == lax.broadcasted_iota(jnp.int32, rows.shape, 1)
    return jnp.sum(jnp.where(pick, rows, 0.0), axis=1, keepdims=True)


def as_row(column):
    size = column.shape[0]
    same = lax.broadcasted_iota(jnp.int32, (size, size), 0)
    same = same == lax.broadcasted_iota(jnp.int32, (size, size), 1)
    return jnp.sum(jnp.where(same, column, 0.0), axis=0, keepdims=True)


VMEM_BYTES = 56 << 20
SHORT = pl.CostEstimate(flops=1, bytes_accessed=1, transcendentals=0)
LONG = pl.CostEstimate(flops=1 << 36, bytes_accessed=1 << 28, transcendentals=0)


def range_state_kernel(width, me_ref, k_ref, v_ref, rate_ref, u_ref, f_ref):
    u = k_ref[...] * v_ref[...]
    u_ref[...] = u
    toks, cols = u.shape
    modes = rate_ref.shape[0]
    count = cols // width
    rate = as_column(rate_ref[...], pl.program_id(0) * count, count)
    rows = rate.shape[0]
    left = (SUB - 1) - lax.broadcasted_iota(jnp.int32, (rows, SUB), 1)
    inject = jnp.exp(-rate * left.astype(F32)).astype(BF16)
    decay = jnp.exp(-rate * SUB)
    sums = dot32(inject, u[:SUB])
    for n in range(1, toks // SUB):
        sums = decay * sums + dot32(inject, u[n * SUB : (n + 1) * SUB])
    sums = jnp.where(own_mask(rows, cols, modes, width), sums, 0.0)
    for to in range(f_ref.shape[0]):
        lag = to - 1 - me_ref[0]
        weight = jnp.exp(-rate * (jnp.maximum(lag, 0) * toks).astype(F32))
        there = (weight * sums).reshape(rows // modes, modes, cols)
        f_ref[to] = jnp.where(lag >= 0, jnp.sum(there, axis=0), 0.0).astype(BF16)


def range_state(me, key_feat, value_feat, rates, seq_size, width):
    toks, chans = key_feat.shape
    modes = rates.shape[0]
    step = 512
    feat = pl.BlockSpec((toks, step), lambda i, p: (0, i))
    return pl.pallas_call(
        functools.partial(range_state_kernel, width),
        grid_spec=pltpu.PrefetchScalarGridSpec(
            num_scalar_prefetch=1,
            grid=(chans // step,),
            in_specs=[feat, feat, pl.BlockSpec(rates.shape, lambda i, p: (0, 0))],
            out_specs=[feat, pl.BlockSpec((seq_size, modes, step), lambda i, p: (0, 0, i))],
        ),
        out_shape=[
            jax.ShapeDtypeStruct((toks, chans), BF16),
            jax.ShapeDtypeStruct((seq_size, modes, chans), BF16),
        ],
        compiler_params=pltpu.CompilerParams(vmem_limit_bytes=VMEM_BYTES),
        cost_estimate=SHORT,
        name="range_state",
    )(me, key_feat, value_feat, rates)


def local_tile(width, tile, u_ref, rate_ref, res_ref, z_ref, rows_ref, taps_ref, split_ref):
    modes, groups = rate_ref.shape[0], TILE // width
    rows = groups * modes
    rate, res = (as_column(r[...], tile * groups, groups) for r in (rate_ref, res_ref))
    rate_row, res_row = as_row(rate), as_row(res)
    rows_ref[0:1, :] = rate_row
    rows_ref[1:2, :] = res_row
    blocks = u_ref.shape[0] // SUB
    lag = 2 * SUB - lax.broadcasted_iota(jnp.int32, (rows, 2 * SUB), 1)
    lag = jnp.where(lag == 2 * SUB, 0, lag)
    terms = jnp.where(lag < SUB, res * jnp.exp(-rate * lag.astype(F32)), 0.0)
    wheel = jnp.sum(terms.reshape(groups, modes, 2 * SUB), axis=1)
    half = SUB // 2
    both = jnp.concatenate([u_ref[n * SUB : (n + 1) * SUB, :] for n in range(blocks)], axis=1)
    lane_group = (lax.broadcasted_iota(jnp.int32, (1, blocks * TILE), 1) % TILE) // width
    for g in range(groups):
        base = jnp.broadcast_to(wheel[g : g + 1], (half, 2 * SUB))
        low = pltpu.roll(base, half, 1, stride=1, stride_axis=0)[:, :SUB].astype(BF16)
        taps_ref[half:, g * SUB : (g + 1) * SUB] = low
        taps_ref[:half, g * SUB : g * SUB + half] = low[:, half:]
        taps_ref[:half, g * SUB + half : (g + 1) * SUB] = jnp.zeros((half, half), BF16)
        split_ref[g * SUB : (g + 1) * SUB, :] = both * (lane_group == g).astype(BF16)

    mask = own_mask(rows, TILE, modes, width)
    left = (SUB - 1) - lax.broadcasted_iota(jnp.int32, (rows, SUB), 1)
    inject = jnp.exp(-rate * left.astype(F32)).astype(BF16)
    sums = dot32(inject, both[:, : (blocks - 1) * TILE])
    decay = jnp.exp(-rate * SUB)
    state, starts = jnp.zeros((rows, TILE), F32), []
    for n in range(blocks - 1):
        own = jnp.where(mask, sums[:, n * TILE : (n + 1) * TILE], 0.0)
        state = decay * state + own
        starts.append(state.astype(BF16))
    after = lax.broadcasted_iota(jnp.int32, (SUB, rows), 0) + 1
    readout = (res_row * jnp.exp(-rate_row * after.astype(F32))).astype(BF16)
    carried = dot32(readout, jnp.concatenate(starts, axis=1))
    z = dot32(taps_ref[...], split_ref[...])
    z_ref[:SUB, :] = z[:, :TILE].astype(BF16)
    for n in range(1, blocks):
        z_ref[n * SUB : (n + 1) * SUB, :] = (
            z[:, n * TILE : (n + 1) * TILE] + carried[:, (n - 1) * TILE : n * TILE]
        ).astype(BF16)


def local_kernel(width, u_ref, rate_ref, res_ref, z_ref, rows_ref, taps_ref, split_ref):
    tiles = u_ref.shape[1] // TILE
    per_tile = rows_ref.shape[1] // tiles
    for t in range(tiles):
        lanes = pl.ds(t * TILE, TILE)
        local_tile(
            width, pl.program_id(0) * tiles + t, u_ref.at[:, lanes], rate_ref, res_ref, z_ref.at[:, lanes],
            rows_ref.at[:, pl.ds(t * per_tile, per_tile)], taps_ref.at[t], split_ref.at[t],
        )


def local_conv(u, rates, residues, width):
    toks, chans = u.shape
    modes = rates.shape[0]
    groups = TILE // width
    rows, tiles = groups * modes, 2
    table = pl.BlockSpec(rates.shape, lambda i: (0, 0))
    feat = pl.BlockSpec((toks, tiles * TILE), lambda i: (0, i))
    return pl.pallas_call(
        functools.partial(local_kernel, width),
        grid=(chans // TILE // tiles,),
        in_specs=[feat, table, table],
        out_specs=[feat, pl.BlockSpec((2, tiles * rows), lambda i: (0, i))],
        out_shape=[
            jax.ShapeDtypeStruct((toks, chans), BF16),
            jax.ShapeDtypeStruct((2, rates.size), F32),
        ],
        scratch_shapes=[
            pltpu.VMEM((tiles, SUB, groups * SUB), BF16),
            pltpu.VMEM((tiles, groups * SUB, toks // SUB * TILE), BF16),
        ],
        compiler_params=pltpu.CompilerParams(vmem_limit_bytes=VMEM_BYTES),
        cost_estimate=SHORT,
        name="local_conv",
    )(u, rates, residues)


def gate_kernel(modes, width, counts, place_ref, z_ref, q_ref, rows_ref, state_ref, *y_refs):
    y_refs = list(zip(y_refs, counts))
    step = pl.program_id(0)
    entering = jnp.sum(state_ref[...].astype(F32), axis=0)
    first = place_ref[step] * SUB + 1
    rows = TILE // width * modes
    mask = own_mask(rows, TILE, modes, width)
    tiles = []
    for tile in range(q_ref.shape[1] // TILE):
        lanes = slice(tile * TILE, (tile + 1) * TILE)
        group = slice(tile * rows, (tile + 1) * rows)
        after = lax.broadcasted_iota(jnp.int32, (SUB, rows), 0) + first
        readout = (
            rows_ref[1:2, group] * jnp.exp(-rows_ref[0:1, group] * after.astype(F32))
        ).astype(BF16)
        spread = jnp.concatenate([entering[:, lanes]] * (TILE // width), axis=0)
        spread = jnp.where(mask, spread, 0.0).astype(BF16)
        z = z_ref[:, lanes].astype(F32) + dot32(readout, spread)
        tiles.append((q_ref[:, lanes].astype(F32) * z).astype(BF16))
    at = 0
    for y_ref, count in y_refs:

        @pl.when((step >= at) & (step < at + count))
        def _():
            y_ref[...] = jnp.concatenate(tiles, axis=1)

        at += count


def gate(places, counts, z, query_feat, rows, states, width):
    modes, chans = states.shape[1], query_feat.shape[1]
    whole = lambda a: pl.BlockSpec(a.shape, lambda i, p: (0,) * a.ndim)
    block = pl.BlockSpec((SUB, chans), lambda i, p: (p[i], 0))

    def result(first, count):
        return pl.BlockSpec((SUB, chans), lambda i, p: (jnp.clip(i - first, 0, count - 1), 0))

    return pl.pallas_call(
        functools.partial(gate_kernel, modes, width, counts),
        grid_spec=pltpu.PrefetchScalarGridSpec(
            num_scalar_prefetch=1,
            grid=(sum(counts),),
            in_specs=[block, block, whole(rows), whole(states)],
            out_specs=[result(sum(counts[:n]), count) for n, count in enumerate(counts)],
        ),
        out_shape=[jax.ShapeDtypeStruct((n * SUB, chans), BF16) for n in counts],
        compiler_params=pltpu.CompilerParams(vmem_limit_bytes=VMEM_BYTES if sum(counts) == 1 else 63 << 20),
        cost_estimate=SHORT,
        name="gate",
    )(places, z, query_feat, rows, states)


def share_kernel(sets, count, adds, *refs):
    near = jnp.concatenate([r[...] for r in refs[:sets]], axis=0)
    far = jnp.concatenate([r[...] for r in refs[sets : 2 * sets]], axis=0)
    weights = refs[2 * sets :][: 2 * count]
    extra, outs = refs[2 * sets + 2 * count :][: len(adds)], refs[2 * sets + 2 * count + len(adds) :]
    rows, cols = outs[0].shape[0], weights[0].shape[1]
    added = {}
    for ref, at in zip(extra, adds):
        for n in range(ref.shape[1] // cols):
            added[at + n] = ref, n * cols
    for i, (wn, wf) in enumerate(zip(weights[:count], weights[count:])):
        total = dot32(near, wn[...]) + dot32(far, wf[...])
        if i in added:
            ref, n = added[i]
            total = total + ref[:, n : n + cols].astype(F32)
        total = total.astype(BF16)
        for j, out in enumerate(outs):
            out[:, i * cols : (i + 1) * cols] = total[j * rows : (j + 1) * rows]


def share(near, far, near_w, far_w, cols, parts=1, adds=(), cost=SHORT):
    depth = near[0][0].shape[1]
    rows = lambda n: pl.BlockSpec((SUB, depth), lambda i: (n, 0))
    part = lambda col: pl.BlockSpec((depth, cols), lambda i: (0, col))
    whole = lambda *shape: pl.BlockSpec(shape, lambda i: (0, 0))
    height, total = len(near) * SUB, cols * len(near_w)
    return pl.pallas_call(
        functools.partial(share_kernel, len(near), len(near_w), [at for _, at in adds]),
        grid=(1,),
        in_specs=[rows(n) for _, n in near + far]
        + [part(col) for _, col in near_w + far_w]
        + [whole(*a.shape) for a, _ in adds],
        out_specs=[whole(height // parts, total)] * parts,
        out_shape=[jax.ShapeDtypeStruct((height // parts, total), BF16)] * parts,
        compiler_params=pltpu.CompilerParams(vmem_limit_bytes=63 << 20),
        cost_estimate=cost,
        name="share",
    )(*[a for a, _ in near + far + near_w + far_w], *[a for a, _ in adds])


def place_kernel(spots, place_ref, *refs):
    out_ref, total_ref, sem = refs[-3:]
    cols = total_ref.shape[2]
    copies = []
    for j, spot in enumerate(spots):
        terms = [refs[i][:, n * cols : (n + 1) * cols] for i, n in spot]
        total = terms[0] if len(terms) == 1 else sum(t.astype(F32) for t in terms).astype(BF16)
        total_ref[j] = total
        to = pl.ds(pl.multiple_of(place_ref[j] * cols, cols), cols)
        copies.append(pltpu.make_async_copy(total_ref.at[j], out_ref.at[:, to], sem.at[j]))
        copies[-1].start()
    for copy in copies:
        copy.wait()


def place(places, terms, cols, all_cols, out=None):
    arrays, spots = [], []
    for group in terms:
        spot = []
        for array, n in group:
            known = [i for i, a in enumerate(arrays) if a is array]
            if not known:
                known = [len(arrays)]
                arrays.append(array)
            spot.append((known[0], n))
        spots.append(spot)
    rows = arrays[0].shape[0]
    specs = [pl.BlockSpec(a.shape, lambda i, p: (0, 0)) for a in arrays]
    alias = {}
    if out is not None:
        alias = {1 + len(arrays): 0}
        arrays.append(out)
        specs.append(pl.BlockSpec(memory_space=pl.ANY))
    return pl.pallas_call(
        functools.partial(place_kernel, spots),
        grid_spec=pltpu.PrefetchScalarGridSpec(
            num_scalar_prefetch=1,
            grid=(1,),
            in_specs=specs,
            out_specs=pl.BlockSpec(memory_space=pl.ANY),
            scratch_shapes=[
                pltpu.VMEM((len(spots), rows, cols), BF16),
                pltpu.SemaphoreType.DMA((len(spots),)),
            ],
        ),
        out_shape=jax.ShapeDtypeStruct((rows, all_cols), BF16),
        input_output_aliases=alias,
        compiler_params=pltpu.CompilerParams(vmem_limit_bytes=63 << 20),
        cost_estimate=SHORT,
        name="place",
    )(places, *arrays)


def arrived_kernel(spots_ref, *refs):
    for i in range(spots_ref.shape[0]):
        refs[-1][i] = spots_ref[i]


def arrived(spots, *arrays):
    smem = pl.BlockSpec(memory_space=pltpu.SMEM)
    return pl.pallas_call(
        arrived_kernel,
        in_specs=[smem] + [pl.BlockSpec(memory_space=pl.ANY)] * len(arrays),
        out_specs=smem,
        out_shape=jax.ShapeDtypeStruct(spots.shape, spots.dtype),
        cost_estimate=LONG,
        name="arrived",
    )(spots, *arrays)


def flip(x, axis, size, bits):
    return lax.ppermute(x, axis, [(i, i ^ bits) for i in range(size)])


def after(x, *others):
    return lax.optimization_barrier((x, *others))[0]


def on_device(seq_size, ch_size, query_feat, key_feat, value_feat, decay_rates, residues, out_weight):
    toks, chans = query_feat.shape
    groups, modes = decay_rates.shape
    width = chans // groups
    piece_cols = out_weight.shape[1]
    all_cols = piece_cols * seq_size
    me = lax.axis_index("seq").astype(jnp.int32)
    plane = lax.axis_index("ch").astype(jnp.int32)
    far_plane = lambda x: flip(x, "ch", ch_size, 2)
    next_plane = lambda x: flip(x, "ch", ch_size, 1)

    rates, residues = decay_rates.T, residues.T
    u, ends = range_state(me.reshape(1), key_feat, value_feat, rates, seq_size, width)
    states = lax.all_to_all(ends, "seq", 0, 0, tiled=True)
    z, rows = local_conv(u, rates, residues, width)

    def gated(slots, counts, *hold):
        places = plane ^ jnp.array(slots, jnp.int32)
        return gate(places, counts, after(z, *hold), query_feat, rows, states, width)

    if seq_size != 8:
        y_3, near, y_2 = gated((3, 1, 0, 2), (1, 2, 1))
        near_w = lax.all_gather(out_weight, "seq", axis=1, tiled=True)
        far_w = lax.all_gather(far_plane(out_weight), "seq", axis=1, tiled=True)
        far_other, far_own = far_plane(y_3), far_plane(y_2)
        near_w, far_w = [(near_w, 0)], [(far_w, 0)]
        (part,) = share([(near, 0)], [(far_other, 0)], near_w, far_w, all_cols)
        (own,) = share([(near, 1)], [(far_own, 0)], near_w, far_w, all_cols)
        return (own.astype(F32) + next_plane(part).astype(F32)).astype(BF16)

    core = lambda x: flip(x, "seq", seq_size, 1)
    pairs = [(s * ch_size + c, (s ^ 1) * ch_size + (c ^ 1)) for s in range(seq_size) for c in range(ch_size)]
    next_cross = lambda x: lax.ppermute(x, ("seq", "ch"), pairs)
    sides = [(2, 4), (4, 2), (6, 6)]

    def over(x, way):
        return lax.ppermute(x, "seq", [(i, i ^ sides[way][i % 2]) for i in range(seq_size)])

    half = piece_cols // 2
    first, second = slice(0, half), slice(half, None)

    n_a = out_weight[:, first]
    f_a = far_plane(n_a)
    n_1 = over(out_weight, 0)
    (y_3,) = gated((3,), (1,), n_1)

    y_far_other = far_plane(after(y_3, f_a))
    f_a = after(f_a, y_3)
    f_a1, f_a2 = over(f_a, 0), over(f_a, 1)
    n_2 = over(after(out_weight, f_a), 1)
    n_b = after(out_weight, y_3)[:, second]
    near, y_2 = gated((1, 0, 2), (2, 1), n_1, f_a, n_b)
    near_sib = core(near)
    there = arrived(me.reshape(1), y_far_other)
    f_a1, f_a2, n_2, _ = lax.optimization_barrier((f_a1, f_a2, n_2, there))
    n_b = after(n_b, y_far_other)

    f_b = far_plane(n_b)
    far_other_sib = core(y_far_other)
    n_3, f_a3 = over(after(n_1, there), 1), over(after(f_a1, there), 1)
    near_w, far_w = [(out_weight, 0), (n_1, 0), (n_2, 0)], [(f_a, 0), (f_a1, 0), (f_a2, 0)]
    near_other, near_own = [(near, 0), (near_sib, 0)], [(near, 1), (near_sib, 1)]
    far_other = [(y_far_other, 0), (far_other_sib, 0)]

    def products(near, far, pieces, **kw):
        return share(near, far, [near_w[i] for i in pieces], [far_w[i] for i in pieces], half, **kw)

    (ready_1,) = products(near_other, far_other, range(3))
    part_1 = next_plane(ready_1)

    f_b, n_3, f_a3 = lax.optimization_barrier((f_b, n_3, f_a3))
    near_w = [(n, h) for h in (0, 1) for n in (out_weight, n_1, n_2, n_3)]
    y_far_own = far_plane(after(y_2, f_b))
    f_b1, f_b2, f_b3 = (over(f_b, way) for way in range(3))
    far_w += [(f_a3, 0), (f_b, 0)]
    (ready_2,) = products(near_other, far_other, range(3, 5))
    part_2 = next_plane(after(ready_2, part_1))
    far_w += [(after(f_b1, y_far_own), 0), (f_b2, 0), (f_b3, 0)]
    mine, other = products(near_other, far_other, range(5, 8), parts=2, cost=LONG)
    part_3 = next_plane(mine), next_cross(other)

    far_own_sib = core(after(y_far_own, mine))
    far_own = [(after(y_far_own, part_2), 0), (far_own_sib, 0)]
    mine, other = products(
        near_own, far_own, range(8), parts=2, adds=[(part_1, 0), (part_2, 3)]
    )
    other = core(other)
    own, cross = [[(mine, n)] for n in range(8)], [[(other, n)] for n in range(8)]
    for n in range(3):
        own[5 + n].append((part_3[0], n))
        cross[5 + n].append((part_3[1], n))

    def spots(s):
        at = me ^ s
        chips = [0, jnp.where(at % 2 == 0, 2, 4), jnp.where(at % 2 == 0, 4, 2), 6]
        return jnp.stack([(at ^ chips[i % 4]) * 2 + i // 4 for i in range(8)])

    early = place(spots(0)[:5], own[:5], half, all_cols)
    at = arrived(jnp.concatenate([spots(0)[5:], spots(1)]), *part_3, early)
    return place(at, own[5:] + cross, half, all_cols, early)


def solution(mesh):
    in_specs = (
        P("seq", "ch"),
        P("seq", "ch"),
        P("seq", "ch"),
        P("ch", None),
        P("ch", None),
        P("ch", "seq"),
    )
    out_specs = P(("seq", "ch"), None)
    body = functools.partial(on_device, mesh.shape["seq"], mesh.shape["ch"])
    return jax.shard_map(
        body, mesh=mesh, in_specs=in_specs, out_specs=out_specs, check_vma=False
    )
```
